32 devices in a mesh: row: 4 (over z), col: 8 (over y, x, core).
Axes of the slice: x: 2, y: 2, z: 4, core: 2. Of those that a mesh axis runs over, the one named last changes fastest.
Arguments:
- tile_data: bfloat16 [4, 8, 256, 128, 128], P('row', 'col')
- tile_rows: int32 [4, 8, 256], P('row', 'col'), may hold values from 0 to 15, as said below
- tile_cols: int32 [4, 8, 256], P('row', 'col'), may hold values from 0 to 31
- tile_count: int32 [4, 8], P('row', 'col'), may hold values from 32 to 256, as said below
- sketch: bfloat16 [32768, 256], P('col')
Outputs:
- range_one: float32 [8192, 256], P(('row', 'col'))
- basis: float32 [8192, 256], P(('row', 'col'))
The draws below stay inside these ranges and needn't reach their ends.
Inputs may be any that keep to these rules, and one draw needn't show every extreme that they name: On each device the pairs (tile_rows, tile_cols) are distinct. A device's live tiles are its first tile_count tiles; the rest are padding.
All inputs are finite; a program needn't handle non-finite values.
Results may differ from the reference program's by a relative error of at most 0.0028.
Values may be sent and summed in bfloat16 or wider, within the bound.
No kernel may reach another device: no remote copies, remote signals or barrier semaphores. Data moves between devices by JAX's collectives and lax.ppermute only.
A program may use at most 128 MiB of HBM per device.

```python
import math
import jax
import jax.numpy as jnp
from jax import lax

TILE = 128
K = 256
RB_G = 16
CB_G = 32
TILES_DEV = 256
ROWS = 8192
COLS = 32768
N_ROW = 4
N_COL = 8


def tile_positions(key):
    base = jax.random.fold_in(key, 11)
    keys = jax.random.split(base, N_ROW * N_COL)
    perms = jax.vmap(lambda k: jax.random.permutation(k, RB_G * CB_G))(keys)[:, :TILES_DEV]
    return perms.reshape(N_ROW, N_COL, TILES_DEV).astype(jnp.int32)


def draw_tile_rows(key, part):
    return (tile_positions(key) // CB_G).astype(jnp.int32)


def draw_tile_cols(key, part):
    return (tile_positions(key) % CB_G).astype(jnp.int32)


def draw_tile_count(key, part):
    total = N_ROW * N_COL
    shifts = jax.random.randint(jax.random.fold_in(key, 21), (total,), 0, 4)
    counts = jnp.floor_divide(TILES_DEV, jnp.left_shift(1, shifts)).astype(jnp.int32)
    top = jax.random.randint(jax.random.fold_in(key, 22), (), 0, total)
    other = (top + 1 + jax.random.randint(jax.random.fold_in(key, 23), (), 0, total - 1)) % total
    counts = counts.at[top].set(TILES_DEV).at[other].set(TILES_DEV // 8)
    return counts.reshape(N_ROW, N_COL).astype(jnp.int32)


def draw_tile_data(key, part):
    shape = (N_ROW, N_COL, TILES_DEV, TILE, TILE)
    first_key = jax.random.fold_in(key, 31)
    second_key = jax.random.fold_in(key, 32)
    values = jax.random.normal(first_key, shape, jnp.float32)
    groups = 1.0 + 2.0 * jnp.arange(N_ROW, dtype=jnp.float32) / max(N_ROW - 1, 1)
    spread = jnp.exp(jax.random.uniform(second_key, (N_ROW, N_COL, TILES_DEV, 1, 1), jnp.float32, -0.7, 0.7))
    fan = TILES_DEV * TILE * N_COL / RB_G
    return (values * groups[:, None, None, None, None] * spread / math.sqrt(fan)).astype(jnp.bfloat16)


def draw_sketch(key, part):
    noise_key = jax.random.fold_in(key, 41)
    common_key = jax.random.fold_in(key, 42)
    weight_key = jax.random.fold_in(key, 43)
    values = jax.random.normal(noise_key, (COLS, K), jnp.float32)
    common = jax.random.normal(common_key, (COLS, 1), jnp.float32)
    column_load = jnp.exp(jax.random.uniform(weight_key, (1, K), jnp.float32, -0.7, 0.0))
    return (values + column_load * common).astype(jnp.bfloat16)


def setup_inputs(seed: int = 0) -> dict:
    streams_of = jax.random.split(jax.random.key(seed), 6)
    return {
        "tile_data": draw_tile_data(jax.random.fold_in(streams_of[5], 71), 0),
        "tile_rows": draw_tile_rows(jax.random.fold_in(streams_of[5], 71), 0),
        "tile_cols": draw_tile_cols(jax.random.fold_in(streams_of[5], 71), 0),
        "tile_count": draw_tile_count(jax.random.fold_in(streams_of[5], 71), 0),
        "sketch": draw_sketch(jax.random.fold_in(streams_of[5], 71), 0),
    }


def apply_tiles(tile_data, out_index, in_index, live, operand, n_out, flip):
    devices = N_ROW * N_COL
    form = 'tba,tbk->tak' if flip else 'tab,tbk->tak'

    def one_device(total, items):
        tiles, target, source, weight = items
        rows = operand[source].astype(jnp.float32)
        product = jnp.einsum(form, tiles.astype(jnp.float32), rows, precision=lax.Precision.HIGHEST)
        product = product * weight[:, None, None]
        return (total.at[target].add(product), None)
    start = jnp.zeros((n_out, TILE, K), jnp.float32)
    items = (tile_data.reshape(devices, TILES_DEV, TILE, TILE), out_index.reshape(devices, TILES_DEV), in_index.reshape(devices, TILES_DEV), live.reshape(devices, TILES_DEV))
    total, unused = lax.scan(one_device, start, items)
    return total

def orthonormal(values):
    gram = jnp.dot(values.T, values, precision=lax.Precision.HIGHEST)
    lower = jnp.linalg.cholesky(gram)
    inverse = lax.linalg.triangular_solve(lower, jnp.eye(K, dtype=jnp.float32), left_side=True, lower=True)
    return jnp.dot(values, inverse.T, precision=lax.Precision.HIGHEST)

def reference(tile_data, tile_rows, tile_cols, tile_count, sketch):
    global_rows = (tile_rows + (jnp.arange(N_ROW, dtype=jnp.int32) * RB_G)[:, None, None]).astype(jnp.int32)
    global_cols = (tile_cols + (jnp.arange(N_COL, dtype=jnp.int32) * CB_G)[None, :, None]).astype(jnp.int32)
    live = (jnp.arange(TILES_DEV, dtype=jnp.int32)[None, None, :] < tile_count[:, :, None]).astype(jnp.float32)
    omega = sketch.reshape(N_COL * CB_G, TILE, K)
    first = apply_tiles(tile_data, global_rows, global_cols, live, omega, N_ROW * RB_G, False).reshape(ROWS, K)
    ortho_float = orthonormal(first)
    range_one = ortho_float * math.sqrt(ROWS)
    ortho_one = ortho_float.astype(jnp.bfloat16)
    cross = apply_tiles(tile_data, global_cols, global_rows, live, ortho_one.reshape(N_ROW * RB_G, TILE, K), N_COL * CB_G, True)
    cross = cross.astype(jnp.bfloat16)
    second = apply_tiles(tile_data, global_rows, global_cols, live, cross, N_ROW * RB_G, False).reshape(ROWS, K)
    return (range_one, orthonormal(second) * math.sqrt(ROWS))
```

```python
import functools
import math

import jax
import jax.numpy as jnp
from jax import lax
from jax.experimental import pallas as pl
from jax.experimental.pallas import tpu as pltpu
from jax.sharding import PartitionSpec as P

RB_G = 16
CB_G = 32
PIECES = 8
LAG = 3
GAIN_MAX = 6.0
DIAG_MIN = 1e-24
DIAG_MAX = 1e30
F32 = jnp.float32
BF16 = jnp.bfloat16
MIB = 1024 * 1024
IN_VMEM = pl.BlockSpec(memory_space=pltpu.VMEM)
IN_SMEM = pl.BlockSpec(memory_space=pltpu.SMEM)
ANYWHERE = pl.BlockSpec(memory_space=pl.ANY)


def tile_product(tiles, out_index, in_index, count, operand, n_out, flip):
    total_tiles = tiles.shape[0]
    width = min(64, total_tiles)
    blocks = total_tiles // width
    form = "tba,tbk->tak" if flip else "tab,tbk->tak"
    targets = jnp.arange(n_out, dtype=jnp.int32)

    def step(number, total):
        start = number * width
        block = lax.dynamic_slice_in_dim(tiles, start, width, 0)
        target = lax.dynamic_slice_in_dim(out_index, start, width, 0)
        source = lax.dynamic_slice_in_dim(in_index, start, width, 0)
        gathered = jnp.take(operand, source, axis=0)
        product = jnp.einsum(form, block, gathered, preferred_element_type=F32)
        weight = (start + jnp.arange(width, dtype=jnp.int32) < count).astype(F32)
        select = (target[None, :] == targets[:, None]).astype(F32) * weight[None, :]
        return total + jnp.einsum("nt,tak->nak", select, product, precision=lax.Precision.HIGHEST)

    start_total = jnp.zeros((n_out, tiles.shape[1], operand.shape[2]), F32)
    return lax.fori_loop(0, blocks, step, start_total)


def gram_of(values):
    return jnp.dot(values.T, values, precision=lax.Precision.HIGHEST)


def orthonormal(values, gram):
    lower = jnp.linalg.cholesky(gram)
    inverse = lax.linalg.triangular_solve(
        lower, jnp.eye(gram.shape[0], dtype=F32), left_side=True, lower=True
    )
    return jnp.dot(values, inverse.T, precision=lax.Precision.HIGHEST)


def plain_way(tiles, row_index, col_index, count, sketch):
    edge = tiles.shape[1]
    width_k = sketch.shape[1]
    scale_rows = math.sqrt(RB_G * edge * lax.axis_size("row"))
    omega = sketch.reshape(CB_G, edge, width_k)
    first = tile_product(tiles, row_index, col_index, count, omega, RB_G, False)
    first = first.reshape(RB_G * edge, width_k)
    whole = lax.psum(first, "col")
    gram = lax.psum(gram_of(whole), "row")
    whole_float = orthonormal(whole, gram)
    share_rows = whole.shape[0] // lax.axis_size("col")
    mine = lax.dynamic_slice_in_dim(whole_float, lax.axis_index("col") * share_rows, share_rows, 0)
    ortho_one = whole_float.astype(BF16).reshape(RB_G, edge, width_k)
    cross = tile_product(tiles, col_index, row_index, count, ortho_one, CB_G, True)
    cross = cross.reshape(CB_G * edge, width_k)
    cross_full = lax.psum(cross, "row").astype(BF16).reshape(CB_G, edge, width_k)
    second = tile_product(tiles, row_index, col_index, count, cross_full, RB_G, False)
    second = second.reshape(RB_G * edge, width_k)
    second_share = lax.psum_scatter(second, "col", scatter_dimension=0, tiled=True)
    gram_two = lax.psum(gram_of(second_share), ("row", "col"))
    return mine * scale_rows, orthonormal(second_share, gram_two) * scale_rows


def call(kernel, outs, operands, specs, name, limit=16, tokens=(), scratch=(), aliases=None, flops=0):
    many = isinstance(outs, (list, tuple))
    nbytes = sum(x.size * x.dtype.itemsize for x in operands)
    return pl.pallas_call(
        kernel,
        out_shape=outs,
        in_specs=list(specs) + [ANYWHERE] * len(tokens),
        out_specs=[IN_VMEM] * len(outs) if many else IN_VMEM,
        scratch_shapes=list(scratch),
        input_output_aliases=aliases or {},
        compiler_params=pltpu.CompilerParams(vmem_limit_bytes=limit * MIB),
        cost_estimate=pl.CostEstimate(flops=flops, bytes_accessed=nbytes, transcendentals=0),
        name=name,
    )(*operands, *tokens)


def exact(a, b, ca=1, cb=0):
    return lax.dot_general(
        a, b, (((ca,), (cb,)), ((), ())), precision=lax.Precision.HIGHEST, preferred_element_type=F32
    )


def dense_kernel(rows_ref, cols_ref, count_ref, tiles_ref, sketch_ref, slab_ref, turned_ref, sem):
    height, width = slab_ref.shape
    edge = tiles_ref.shape[1]

    def clear(i, carry):
        slab_ref[pl.ds(pl.multiple_of(i * edge, edge), edge), :] = jnp.zeros((edge, width), slab_ref.dtype)
        return carry

    lax.fori_loop(0, height // edge, clear, 0)
    count = count_ref[0]

    def place(t):
        r = pl.multiple_of(rows_ref[t] * edge, edge)
        c = pl.multiple_of(cols_ref[t] * edge, edge)
        return pltpu.make_async_copy(
            tiles_ref.at[t], slab_ref.at[pl.ds(r, edge), pl.ds(c, edge)], sem
        )

    def start(t, carry):
        place(t).start()
        return carry

    def finish(t, carry):
        place(t).wait()
        return carry

    lax.fori_loop(0, count, start, 0)
    for j in range(width // edge):
        turned_ref[:, j * edge : (j + 1) * edge] = sketch_ref[j * edge : (j + 1) * edge, :].T
    lax.fori_loop(0, count, finish, 0)


def first_kernel(slab_ref, turned_ref, out_ref):
    share = out_ref.shape[2]

    def step(i, carry):
        block = slab_ref[pl.ds(pl.multiple_of(i * share, share), share), :]
        out_ref[i] = lax.dot_general(
            turned_ref[...], block, (((1,), (1,)), ((), ())), preferred_element_type=F32
        )
        return carry

    lax.fori_loop(0, out_ref.shape[0], step, 0)


def split_kernel(even_ref, odd_ref, out_ref):
    pairs, k, share = even_ref.shape
    for i in range(pairs):
        for parity, ref in ((0, even_ref), (1, odd_ref)):
            value = ref[i]
            high = value.astype(BF16)
            low = (value - high.astype(F32)).astype(BF16)
            at = (2 * i + parity) * share
            out_ref[:k, at : at + share] = high
            out_ref[k:, at : at + share] = low


def gram_kernel(*refs, n):
    out_ref = refs[-1]
    total = None
    for ref in refs[:n]:
        for i in range(ref.shape[0]):
            value = ref[i]
            term = exact(value, value, 1, 1)
            total = term if total is None else total + term
    out_ref[...] = total


def cross_kernel(split_ref, slab_ref, out_ref, *, start):
    k, width = out_ref.shape
    both = jnp.dot(split_ref[...], slab_ref[:, start : start + width], preferred_element_type=F32)
    out_ref[...] = both[:k] + both[k:]


def pick_kernel(role_ref, *refs, n, has_received):
    received = refs[n] if has_received else None
    out_ref = refs[n + has_received] if False else refs[-1]
    for role in range(n):

        @pl.when(role_ref[0] == role)
        def _(role=role):
            value = refs[role][...]
            if has_received and role > 0:
                value = value + received[...].astype(F32)
            out_ref[...] = value.astype(out_ref.dtype)


def send_on_kernel(role_ref, *refs, n):
    for role in range(n):

        @pl.when(role_ref[0] == role)
        def _(role=role):
            refs[-1][...] = (refs[role][...] + refs[n][...].astype(F32)).astype(refs[-1].dtype)


def second_kernel(role_ref, own_ref, *refs, n, start, has_base, ntok):
    even_refs, odd_refs = refs[:n], refs[n : 2 * n]
    base_ref = refs[2 * n + 1] if has_base else None
    slab_ref = refs[2 * n]
    at = 2 * n + 1 + has_base + ntok
    out_ref, total_ref = refs[at], refs[at + 1]
    k, width = own_ref.shape
    for role in range(n):

        @pl.when(role_ref[0] == role)
        def _(role=role):
            total = own_ref[...] + even_refs[role][...].astype(F32) + odd_refs[role][...].astype(F32)
            high = total.astype(BF16)
            total_ref[:k, :] = high
            total_ref[k:, :] = (total - high.astype(F32)).astype(BF16)

    share = out_ref.shape[2]
    for i in range(out_ref.shape[0]):
        block = slab_ref[i * share : (i + 1) * share, start : start + width]
        both = lax.dot_general(
            total_ref[...], block, (((1,), (1,)), ((), ())), preferred_element_type=F32
        )
        value = both[:k] + both[k:]
        out_ref[i] = base_ref[i] + value if has_base else value


def chol_inverse(a, step):
    n = a.shape[0]
    rows = lax.broadcasted_iota(jnp.int32, (n, n), 0)
    lanes = lax.broadcasted_iota(jnp.int32, (n, n), 1)
    lane = lax.broadcasted_iota(jnp.int32, (1, n), 1)
    pivots = jnp.ones((1, n), F32)
    done = []
    for k in range(0, n, step):
        m = a.shape[0]
        cols = [jnp.broadcast_to(a[:, k + j : k + j + 1], (m, n)) for j in range(step)]
        s = [[cols[q][j : j + 1, :] for q in range(step)] for j in range(step)]
        r = [a[j : j + 1, :] for j in range(step)]
        update = None
        for j in range(step):
            inverse = 1.0 / s[j][j]
            pivots = jnp.where(lane == k + j, s[j][j], pivots)
            row = r[j] + jnp.where(lane == k + j, s[j][j], 0.0)
            for q in range(j + 1, step):
                factor = s[q][j] * inverse
                r[q] = r[q] - factor * row
                for p in range(j + 1, step):
                    s[q][p] = s[q][p] - factor * s[j][p]
            column = cols[j] * inverse
            for q in range(j + 1, step):
                cols[q] = cols[q] - column * s[j][q]
            update = column * row if update is None else update + column * row
        done.extend(r)
        if m > step:
            a = a[step:] - update[step:]
    full = jnp.concatenate(done, 0)
    root = jnp.broadcast_to(lax.rsqrt(pivots), (n, n))
    by_row = jnp.sum(jnp.where(rows == lanes, root, 0.0), axis=1, keepdims=True)
    return jnp.where(lanes <= rows, full * (1.0 / pivots) * by_row, 0.0)


def finish_kernel(gram_ref, share_ref, out_ref, check_ref, inverse_ref, *, scale):
    k = gram_ref.shape[0]
    h = k // 2
    gram = gram_ref[...]
    top = chol_inverse(gram[:h, :h], 8)
    side = exact(top, gram[:h, h:])
    low = chol_inverse(gram[h:, h:] - exact(side, side, 0, 0), 8)
    inverse_ref[:h, :h] = top
    inverse_ref[:h, h:] = jnp.zeros((h, k - h), F32)
    inverse_ref[h:, :h] = -exact(exact(low, side, 1, 1), top)
    inverse_ref[h:, h:] = low
    inverse = inverse_ref[...]
    out_ref[...] = exact(share_ref[...], inverse, 0, 1) * scale
    rows = lax.broadcasted_iota(jnp.int32, (k, k), 0)
    lanes = lax.broadcasted_iota(jnp.int32, (k, k), 1)
    diagonal = jnp.sum(jnp.where(rows == lanes, gram, 0.0), axis=0, keepdims=True)
    gain = jnp.sum(jnp.sum(inverse * inverse * diagonal, axis=1, keepdims=True), axis=0, keepdims=True) / k
    least = jnp.min(diagonal, axis=1, keepdims=True)
    most = jnp.max(diagonal, axis=1, keepdims=True)
    good = (gain < GAIN_MAX) & (least > DIAG_MIN) & (most < DIAG_MAX)
    check_ref[...] = jnp.broadcast_to(jnp.where(good, 1.0, 0.0), check_ref.shape)


def tie(value, tokens):
    return lax.optimization_barrier((value, *tokens))[0] if tokens else value


def swap(value, axis, bit):
    n = lax.axis_size(axis)
    return lax.ppermute(value, axis, [(i, i ^ bit) for i in range(n)])


def bits_of(n, first):
    bits = []
    bit = first
    while bit < n:
        bits.append(bit)
        bit *= 2
    return bits


def parity_halves(blocks, parity):
    pairs = blocks.reshape(blocks.shape[0] // 2, 2, *blocks.shape[1:])
    keep = lax.dynamic_index_in_dim(pairs, parity, 1, keepdims=False)
    give = lax.dynamic_index_in_dim(pairs, 1 - parity, 1, keepdims=False)
    return keep, give


def sum_over_chips(blocks):
    n = lax.axis_size("col")
    bits = bits_of(n, 2)
    h = blocks.shape[1] // 2
    halves = [blocks[:, :h], blocks[:, h:]]
    for level in range(len(bits)):
        moved = [swap(half, "col", bits[(level + t) % len(bits)]) for t, half in enumerate(halves)]
        halves = [half + other for half, other in zip(halves, moved)]
    return jnp.concatenate(halves, axis=1)


def gram_over_rows(half):
    for bit in bits_of(lax.axis_size("row"), 1):
        half = half + swap(half, "row", bit)
    return half


def join_cores(half, parity):
    other = swap(half, "col", 1)
    low = jnp.where(parity == 0, half, other)
    high = jnp.where(parity == 0, other, half)
    return low, high


def scan_rows(split, slab, k, width, shares, share):
    n = lax.axis_size("row")
    roles = n // 2
    i = lax.axis_index("row")
    even = (i % 2) == 0
    hop_even = jnp.where(even, i, n - 1 - i)
    hop_odd = jnp.where(even, n - 1 - i, i)
    role_even = (hop_even // 2).astype(jnp.int32)[None]
    role_odd = ((hop_odd - 1) // 2).astype(jnp.int32)[None]
    role_sum = (jnp.where(even, n - 2 - i, i - 1) // 2).astype(jnp.int32)[None]
    pairs_even = [(j, j ^ 1) for j in range(n)]
    pairs_odd = [(j, j + 1) for j in range(1, n - 1, 2)] + [(j + 1, j) for j in range(1, n - 1, 2)]
    m = PIECES
    piece = width // m
    own = {}
    tokens = ()

    def own_of(q):
        q = min(max(q, 0), m - 1)
        if q not in own:
            own[q] = call(
                functools.partial(cross_kernel, start=q * piece),
                jax.ShapeDtypeStruct((k, piece), F32),
                (split, slab),
                (IN_VMEM, IN_VMEM),
                "cross_piece",
                limit=12,
                flops=4 * k * slab.shape[0] * piece,
            )
        return own[q]

    sent_even, sent_odd = {}, {}
    n_even = m + (roles - 1) * LAG
    n_odd = m + (roles - 2) * LAG if roles > 1 else 0

    def send_even(s):
        nonlocal tokens
        if s >= n_even or s in sent_even:
            return
        owns = [own_of(s - role * LAG) for role in range(roles)]
        received = sent_odd.get(s - LAG)
        operands = (role_even, *owns) + ((received,) if received is not None else ())
        value = call(
            functools.partial(pick_kernel, n=roles, has_received=received is not None),
            jax.ShapeDtypeStruct((k, piece), BF16),
            operands,
            (IN_SMEM,) + (IN_VMEM,) * (len(operands) - 1),
            "send_even",
            limit=8,
            tokens=tokens,
        )
        tokens = (value,)
        sent_even[s] = lax.ppermute(value, "row", pairs_even)

    def send_odd(s):
        nonlocal tokens
        if not 0 <= s < n_odd:
            return
        owns = [own_of(s - role * LAG) for role in range(roles - 1)]
        value = call(
            functools.partial(send_on_kernel, n=roles - 1),
            jax.ShapeDtypeStruct((k, piece), BF16),
            (jnp.minimum(role_odd, roles - 2), *owns, sent_even[s]),
            (IN_SMEM,) + (IN_VMEM,) * roles,
            "send_odd",
            limit=8,
            tokens=tokens,
        )
        tokens = (value,)
        sent_odd[s] = lax.ppermute(value, "row", pairs_odd)

    second = None
    nothing = jnp.zeros((k, piece), BF16)

    def product(q):
        nonlocal tokens, second
        if not 0 <= q < m:
            return
        evens = [sent_even[q + role * LAG] for role in range(roles)]
        odds = [odd_for(q, role) for role in range(roles)]
        base = () if second is None else (second,)
        ntok = len(tokens)
        operands = (role_sum, own_of(q), *evens, *odds, slab, *base)
        second = call(
            functools.partial(
                second_kernel, n=roles, start=q * piece, has_base=bool(base), ntok=ntok
            ),
            jax.ShapeDtypeStruct((shares, k, share), F32),
            operands,
            (IN_SMEM,) + (IN_VMEM,) * (len(operands) - 1),
            "second_piece",
            limit=16,
            tokens=tokens,
            scratch=(pltpu.VMEM((2 * k, piece), BF16),),
            aliases={len(operands) - 1: 0} if base else None,
            flops=4 * k * slab.shape[0] * piece,
        )
        tokens = (second,)

    def odd_for(q, role):
        oh = n - 3 - 2 * role
        if oh < 0:
            return nothing
        return sent_odd[q + ((oh - 1) // 2) * LAG]

    send_even(0)
    for s in range(n_even):
        need = s + 1 - LAG
        if need < 0 or need in sent_odd or need >= n_odd:
            send_even(s + 1)
        send_odd(s)
        send_even(s + 1)
        product(s - (roles - 1) * LAG)
    return second


def body(tile_data, tile_rows, tile_cols, tile_count, sketch):
    tiles = tile_data[0, 0]
    row_index = tile_rows[0, 0]
    col_index = tile_cols[0, 0]
    count = tile_count[0]
    edge = tiles.shape[1]
    k = sketch.shape[1]
    height, width = RB_G * edge, CB_G * edge
    shares = lax.axis_size("col")
    share = height // shares
    scale = math.sqrt(height * lax.axis_size("row"))
    me = lax.axis_index("col")
    core = me % 2

    with jax.named_scope("dense_block"):
        slab, turned = call(
            dense_kernel,
            [jax.ShapeDtypeStruct((height, width), BF16), jax.ShapeDtypeStruct((k, width), BF16)],
            (row_index, col_index, count, tiles, sketch),
            (IN_SMEM, IN_SMEM, IN_SMEM, ANYWHERE, IN_VMEM),
            "dense_block",
            limit=24,
            scratch=(pltpu.SemaphoreType.DMA,),
        )
    with jax.named_scope("first"):
        part = call(
            first_kernel,
            jax.ShapeDtypeStruct((shares, k, share), F32),
            (slab, turned),
            (IN_VMEM, IN_VMEM),
            "first",
            limit=12,
            flops=2 * height * width * k,
        )
        keep, give = parity_halves(part, core)
        chip = keep + swap(give, "col", 1)
        mine = sum_over_chips(chip)
        even, odd = join_cores(mine, core)
        split = call(
            split_kernel,
            jax.ShapeDtypeStruct((2 * k, height), BF16),
            (even, odd),
            (IN_VMEM, IN_VMEM),
            "split",
            limit=12,
        )
    with jax.named_scope("cross_second"):
        second = scan_rows(split, slab, k, width, shares, share)
    finish = functools.partial(finish_kernel, scale=scale)
    outs = [jax.ShapeDtypeStruct((share, k), F32), jax.ShapeDtypeStruct((8, 128), F32)]
    inverse_scratch = (pltpu.VMEM((k, k), F32),)
    with jax.named_scope("second_sum"):
        keep, give = parity_halves(second, core)
        chip = keep + swap(give, "col", 1)
        second_mine = sum_over_chips(chip)
    with jax.named_scope("range_one"):
        gram = call(
            functools.partial(gram_kernel, n=2),
            jax.ShapeDtypeStruct((k, k), F32),
            (even, odd),
            (IN_VMEM, IN_VMEM),
            "gram_one",
            limit=12,
        )
        half = lax.dynamic_slice_in_dim(gram, core * (k // 2), k // 2, 0)
        half = gram_over_rows(tie(half, (second,)))
        gram = jnp.concatenate(join_cores(half, core), axis=0)
        block = lax.dynamic_index_in_dim(mine, me // 2, 0, keepdims=False)
        range_one, check_one = call(
            finish, outs, (gram, block), (IN_VMEM, IN_VMEM), "range_one", limit=12, scratch=inverse_scratch
        )
    with jax.named_scope("basis"):
        gram = call(
            functools.partial(gram_kernel, n=1),
            jax.ShapeDtypeStruct((k, k), F32),
            (second_mine,),
            (IN_VMEM,),
            "gram_two",
            limit=12,
        )
        h = k // 2
        keep = lax.dynamic_slice_in_dim(gram, core * h, h, 0)
        give = lax.dynamic_slice_in_dim(gram, (1 - core) * h, h, 0)
        half = gram_over_rows(keep + swap(give, "col", 1))
        gram = jnp.concatenate(join_cores(half, core), axis=0)
        block = lax.dynamic_index_in_dim(second_mine, me // 2, 0, keepdims=False)
        basis, check_two = call(
            finish, outs, (gram, block), (IN_VMEM, IN_VMEM), "basis", limit=12, scratch=inverse_scratch
        )
    safe = (check_one[0, 0] > 0.5) & (check_two[0, 0] > 0.5)
    return lax.cond(
        safe,
        lambda: (range_one, basis),
        lambda: plain_way(tiles, row_index, col_index, tile_count[0, 0], sketch),
    )


def solution(mesh):
    placed = (
        P("row", "col", None, None, None),
        P("row", "col", None),
        P("row", "col", None),
        P("row", "col"),
        P("col", None),
    )
    return jax.shard_map(
        body,
        mesh=mesh,
        in_specs=placed,
        out_specs=(P(("row", "col"), None), P(("row", "col"), None)),
        check_vma=False,
    )
```

```python
import functools
import math

import jax
import jax.numpy as jnp
from jax import lax
from jax.experimental import pallas as pl
from jax.experimental.pallas import tpu as pltpu
from jax.sharding import PartitionSpec as P

RB_G = 16
CB_G = 32
CHUNKS = 1
PIECES = 8
LAG = 3
CODE_MAX = 32700.0
GAIN_MAX = 6.0
DIAG_MIN = 1e-24
DIAG_MAX = 1e30
F32 = jnp.float32
BF16 = jnp.bfloat16
MIB = 1024 * 1024
SMALL = pl.CostEstimate(flops=1, bytes_accessed=1, transcendentals=0)
IN_VMEM = pl.BlockSpec(memory_space=pltpu.VMEM)
IN_SMEM = pl.BlockSpec(memory_space=pltpu.SMEM)
ANYWHERE = pl.BlockSpec(memory_space=pl.ANY)
IN_HBM = pl.BlockSpec(memory_space=pltpu.HBM)


def tile_product(tiles, out_index, in_index, count, operand, n_out, flip):
    total_tiles = tiles.shape[0]
    width = min(64, total_tiles)
    blocks = total_tiles // width
    form = "tba,tbk->tak" if flip else "tab,tbk->tak"
    targets = jnp.arange(n_out, dtype=jnp.int32)

    def step(number, total):
        start = number * width
        block = lax.dynamic_slice_in_dim(tiles, start, width, 0)
        target = lax.dynamic_slice_in_dim(out_index, start, width, 0)
        source = lax.dynamic_slice_in_dim(in_index, start, width, 0)
        gathered = jnp.take(operand, source, axis=0)
        product = jnp.einsum(form, block, gathered, preferred_element_type=F32)
        weight = (start + jnp.arange(width, dtype=jnp.int32) < count).astype(F32)
        select = (target[None, :] == targets[:, None]).astype(F32) * weight[None, :]
        return total + jnp.einsum("nt,tak->nak", select, product, precision=lax.Precision.HIGHEST)

    start_total = jnp.zeros((n_out, tiles.shape[1], operand.shape[2]), F32)
    return lax.fori_loop(0, blocks, step, start_total)


def gram_of(values):
    return jnp.dot(values.T, values, precision=lax.Precision.HIGHEST)


def orthonormal(values, gram):
    lower = jnp.linalg.cholesky(gram)
    inverse = lax.linalg.triangular_solve(
        lower, jnp.eye(gram.shape[0], dtype=F32), left_side=True, lower=True
    )
    return jnp.dot(values, inverse.T, precision=lax.Precision.HIGHEST)


def sum_over(value, axis):
    n = lax.axis_size(axis)
    if n & (n - 1):
        return lax.psum(value, axis)
    bit = 1
    while bit < n:
        value = value + lax.ppermute(value, axis, [(i, i ^ bit) for i in range(n)])
        bit *= 2
    return value


def plain_way(tiles, row_index, col_index, count, sketch):
    edge = tiles.shape[1]
    width_k = sketch.shape[1]
    scale_rows = math.sqrt(RB_G * edge * lax.axis_size("row"))
    omega = sketch.reshape(CB_G, edge, width_k)
    first = tile_product(tiles, row_index, col_index, count, omega, RB_G, False)
    first = first.reshape(RB_G * edge, width_k)
    whole = sum_over(first, "col")
    gram = sum_over(gram_of(whole), "row")
    whole_float = orthonormal(whole, gram)
    share_rows = whole.shape[0] // lax.axis_size("col")
    mine = lax.dynamic_slice_in_dim(whole_float, lax.axis_index("col") * share_rows, share_rows, 0)
    ortho_one = whole_float.astype(BF16).reshape(RB_G, edge, width_k)
    cross = tile_product(tiles, col_index, row_index, count, ortho_one, CB_G, True)
    cross = cross.reshape(CB_G * edge, width_k)
    cross_full = sum_over(cross, "row").astype(BF16).reshape(CB_G, edge, width_k)
    second = tile_product(tiles, row_index, col_index, count, cross_full, RB_G, False)
    second = second.reshape(RB_G * edge, width_k)
    second = sum_over(second, "col")
    second_share = lax.dynamic_slice_in_dim(second, lax.axis_index("col") * share_rows, share_rows, 0)
    gram_two = sum_over(gram_of(second), "row")
    return mine * scale_rows, orthonormal(second_share, gram_two) * scale_rows


class Order:
    def __init__(self):
        self.token = None

    def run(self, kernel, outs, operands, specs, name, limit=12, scratch=(), aliases=None):
        n_in, n_out = len(operands), len(outs)
        tokens = () if self.token is None else (self.token,)

        def ordered(*refs):
            results = refs[n_in + len(tokens) :]
            results[n_out][...] = jnp.zeros(results[n_out].shape, F32)
            kernel(*refs[:n_in], *results[:n_out], *results[n_out + 1 :])

        *results, self.token = pl.pallas_call(
            ordered,
            out_shape=[*outs, jax.ShapeDtypeStruct((8, 128), F32)],
            in_specs=list(specs) + [ANYWHERE] * len(tokens),
            out_specs=[IN_VMEM] * (n_out + 1),
            scratch_shapes=list(scratch),
            input_output_aliases=aliases or {},
            compiler_params=pltpu.CompilerParams(vmem_limit_bytes=limit * MIB),
            cost_estimate=SMALL,
            name=name,
        )(*operands, *tokens)
        return results


def exact(a, b, ca=1, cb=0):
    return lax.dot_general(
        a, b, (((ca,), (cb,)), ((), ())), precision=lax.Precision.HIGHEST, preferred_element_type=F32
    )


def dense_first_kernel(
    core_ref, rows_ref, cols_ref, count_ref, tiles_ref, sketch_ref, *refs, chunks, pieces
):
    slabs, outs = refs[:pieces], refs[pieces : pieces + 2 * chunks]
    slab_ref, turned_ref, sem, out_sems = refs[pieces + 2 * chunks :]
    _, height, piece = slab_ref.shape
    edge = tiles_ref.shape[1]
    per = piece // edge

    def clear(i, carry):
        for p in range(pieces):
            slab_ref[p, pl.ds(pl.multiple_of(i * edge, edge), edge), :] = jnp.zeros((edge, piece), slab_ref.dtype)
        return carry

    lax.fori_loop(0, height // edge, clear, 0)
    count = count_ref[0]

    def place(t):
        r = pl.multiple_of(rows_ref[t] * edge, edge)
        c = cols_ref[t]
        at = pl.multiple_of(lax.rem(c, per) * edge, edge)
        return pltpu.make_async_copy(
            tiles_ref.at[t], slab_ref.at[lax.div(c, per), pl.ds(r, edge), pl.ds(at, edge)], sem
        )

    def start(t, carry):
        place(t).start()
        return carry

    def finish(t, carry):
        place(t).wait()
        return carry

    lax.fori_loop(0, count, start, 0)
    for j in range(pieces * per):
        turned_ref[:, j * edge : (j + 1) * edge] = sketch_ref[j * edge : (j + 1) * edge, :].T
    lax.fori_loop(0, count, finish, 0)
    writes = [
        pltpu.make_async_copy(slab_ref.at[p], slabs[p], out_sems.at[p]) for p in range(pieces)
    ]
    for write in writes:
        write.start()
    core = core_ref[0]
    pairs, k, share = outs[0].shape

    def step(j, carry):
        for side in range(2):
            i = 2 * j + (core if side == 0 else 1 - core)
            at = pl.ds(pl.multiple_of(i * share, share), share)
            value = None
            for p in range(pieces):
                block = slab_ref[p, at, :]
                term = lax.dot_general(
                    turned_ref[:, p * piece : (p + 1) * piece],
                    block,
                    (((1,), (1,)), ((), ())),
                    preferred_element_type=F32,
                )
                value = term if value is None else value + term
            for c in range(chunks):
                outs[2 * c + side][j] = value[c * k : (c + 1) * k]
        return carry

    lax.fori_loop(0, pairs, step, 0)
    for write in writes:
        write.wait()


def split_kernel(core_ref, mine_ref, other_ref, out_ref):
    pairs, k, share = mine_ref.shape
    core = core_ref[0]
    for i in range(pairs):
        for parity, ref in ((core, mine_ref), (1 - core, other_ref)):
            value = ref[i]
            high = value.astype(BF16)
            at = pl.ds(pl.multiple_of((2 * i + parity) * share, share), share)
            out_ref[:k, at] = high
            out_ref[k:, at] = (value - high.astype(F32)).astype(BF16)


def gram_one_kernel(*refs, chunks):
    out_ref = refs[-1]

    def of(lists, i):
        rows = jnp.concatenate([ref[i] for ref in lists], axis=0)
        return exact(rows, rows, 1, 1)

    out_ref[...] = jnp.zeros(out_ref.shape, F32)

    def step(i, carry):
        out_ref[...] += of(refs[:chunks], i) + of(refs[chunks : 2 * chunks], i)
        return carry

    lax.fori_loop(0, refs[0].shape[0], step, 0)


def gram_kernel(*refs, n):
    out_ref = refs[-1]
    k = out_ref.shape[0]
    out_ref[...] = jnp.zeros(out_ref.shape, F32)

    def step(i, carry):
        rows = jnp.concatenate([ref[i] for ref in refs[:n]], axis=0)
        out_ref[...] += exact(rows[(n - 1) * k :], rows, 1, 1)
        return carry

    lax.fori_loop(0, refs[0].shape[0], step, 0)


def cross_kernel(split_ref, slab_ref, out_ref):
    k, width = out_ref.shape
    step = min(512, width)

    def part(i, carry):
        at = pl.ds(pl.multiple_of(i * step, step), step)
        both = jnp.dot(split_ref[...], slab_ref[:, at], preferred_element_type=F32)
        out_ref[:, at] = both[:k] + both[k:]
        return carry

    lax.fori_loop(0, width // step, part, 0)


def pick_kernel(role_ref, *refs, n, has_received):
    received = refs[n] if has_received else None
    out_ref = refs[-1]
    for role in range(n):

        @pl.when(role_ref[0] == role)
        def _(role=role):
            value = refs[role][...]
            if has_received and role > 0:
                value = value + received[...].astype(F32)
            out_ref[...] = value.astype(out_ref.dtype)


def send_on_kernel(role_ref, *refs, n):
    for role in range(n):

        @pl.when(role_ref[0] == role)
        def _(role=role):
            refs[-1][...] = (refs[role][...] + refs[n][...].astype(F32)).astype(refs[-1].dtype)


def second_kernel(core_ref, role_ref, own_ref, slab_ref, *refs, n, has_base):
    even_refs, odd_refs = refs[:n], refs[n : 2 * n]
    bases = refs[2 * n : 2 * n + 2] if has_base else (None, None)
    at = 2 * n + 2 * has_base
    outs, total_ref = refs[at : at + 2], refs[at + 2]
    k = own_ref.shape[0]
    pairs, _, share = outs[0].shape
    core = core_ref[0]
    for role in range(n):

        @pl.when(role_ref[0] == role)
        def _(role=role):
            total = own_ref[...] + even_refs[role][...].astype(F32) + odd_refs[role][...].astype(F32)
            high = total.astype(BF16)
            total_ref[:k, :] = high
            total_ref[k:, :] = (total - high.astype(F32)).astype(BF16)

    def step(j, carry):
        for side in range(2):
            i = 2 * j + (core if side == 0 else 1 - core)
            block = slab_ref[pl.ds(pl.multiple_of(i * share, share), share), :]
            both = lax.dot_general(
                total_ref[...], block, (((1,), (1,)), ((), ())), preferred_element_type=F32
            )
            value = both[:k] + both[k:]
            outs[side][j] = bases[side][j] + value if has_base else value
        return carry

    lax.fori_loop(0, pairs, step, 0, unroll=2)


def add_kernel(*refs, n):
    for i in range(n):
        refs[2 * n + i][...] = refs[2 * i][...] + refs[2 * i + 1][...]


def encode(blocks, low_ref, high_ref):
    h = low_ref.shape[0]
    share = blocks[0].shape[1]
    most = functools.reduce(jnp.maximum, [jnp.max(jnp.abs(v), axis=1, keepdims=True) for v in blocks])
    power = jnp.ceil(jnp.log2(jnp.maximum(most, 1e-36) * (1.0 / CODE_MAX)))
    inverse = jnp.exp2(-power)
    for i, v in enumerate(blocks):
        code = jnp.round(v * inverse).astype(jnp.int32).astype(jnp.int16)
        at = slice(i * share, (i + 1) * share)
        low_ref[:, at] = code[:h]
        high_ref[:, at] = code[h:]
    tail = slice(len(blocks) * share, low_ref.shape[1])
    width = low_ref.shape[1] - len(blocks) * share
    power = jnp.broadcast_to(power, (2 * h, width)).astype(jnp.int32).astype(jnp.int16)
    low_ref[:, tail] = power[:h]
    high_ref[:, tail] = power[h:]


def decode(ref, pairs, share):
    power = ref[:, pairs * share : pairs * share + 128].astype(jnp.int32).astype(F32)
    factor = jnp.exp2(jnp.max(power, axis=1, keepdims=True))
    return [
        ref[:, i * share : (i + 1) * share].astype(jnp.int32).astype(F32) * factor for i in range(pairs)
    ]


def code_first_kernel(a_ref, b_ref, low_ref, high_ref):
    encode([a_ref[i] + b_ref[i] for i in range(a_ref.shape[0])], low_ref, high_ref)


def decoded_sums(refs, pairs, share):
    low, low_more, high, high_more = [decode(ref, pairs, share) for ref in refs]
    return [
        jnp.concatenate([low[i] + low_more[i], high[i] + high_more[i]], axis=0) for i in range(pairs)
    ]


def code_next_kernel(*refs, pairs, share):
    encode(decoded_sums(refs[:4], pairs, share), refs[4], refs[5])


def code_last_kernel(*refs):
    out_ref = refs[4]
    for i, v in enumerate(decoded_sums(refs[:4], out_ref.shape[0], out_ref.shape[2])):
        out_ref[i] = v


def keep_give_kernel(core_ref, value_ref, keep_ref, give_ref):
    h = keep_ref.shape[0]
    core = core_ref[0]
    keep_ref[...] = value_ref[pl.ds(pl.multiple_of(core * h, h), h), :]
    give_ref[...] = value_ref[pl.ds(pl.multiple_of((1 - core) * h, h), h), :]


def whole_of(core_ref, mine, other):
    core = core_ref[0] == 0
    return jnp.concatenate([jnp.where(core, mine, other), jnp.where(core, other, mine)], axis=0)


def chol_inverse(a, step):
    n = a.shape[0]
    rows = lax.broadcasted_iota(jnp.int32, (n, n), 0)
    lanes = lax.broadcasted_iota(jnp.int32, (n, n), 1)
    lane = lax.broadcasted_iota(jnp.int32, (1, n), 1)
    pivots = jnp.ones((1, n), F32)
    done = []
    for k in range(0, n, step):
        m = a.shape[0]
        cols = [jnp.broadcast_to(a[:, k + j : k + j + 1], (m, n)) for j in range(step)]
        s = [[cols[q][j : j + 1, :] for q in range(step)] for j in range(step)]
        r = [a[j : j + 1, :] for j in range(step)]
        update = None
        for j in range(step):
            inverse = 1.0 / s[j][j]
            pivots = jnp.where(lane == k + j, s[j][j], pivots)
            row = r[j] + jnp.where(lane == k + j, s[j][j], 0.0)
            for q in range(j + 1, step):
                factor = s[q][j] * inverse
                r[q] = r[q] - factor * row
                for p in range(j + 1, step):
                    s[q][p] = s[q][p] - factor * s[j][p]
            column = cols[j] * inverse
            for q in range(j + 1, step):
                cols[q] = cols[q] - column * s[j][q]
            update = column * row if update is None else update + column * row
        done.extend(r)
        if m > step:
            a = a[step:] - update[step:]
    full = jnp.concatenate(done, 0)
    root = jnp.broadcast_to(lax.rsqrt(pivots), (n, n))
    by_row = jnp.sum(jnp.where(rows == lanes, root, 0.0), axis=1, keepdims=True)
    return jnp.where(lanes <= rows, full * (1.0 / pivots) * by_row, 0.0)


def check_of(squares, diagonals):
    k = sum(d.shape[1] for d in diagonals)
    gain = jnp.sum(jnp.sum(squares, axis=1, keepdims=True), axis=0, keepdims=True) / k
    good = gain < GAIN_MAX
    for diagonal in diagonals:
        good &= (jnp.min(diagonal, axis=1, keepdims=True) > DIAG_MIN) & (
            jnp.max(diagonal, axis=1, keepdims=True) < DIAG_MAX
        )
    return jnp.broadcast_to(jnp.where(good, 1.0, 0.0), (8, 128))


def diagonal_of(gram):
    k = gram.shape[0]
    rows = lax.broadcasted_iota(jnp.int32, (k, k), 0)
    lanes = lax.broadcasted_iota(jnp.int32, (k, k), 1)
    return jnp.sum(jnp.where(rows == lanes, gram, 0.0), axis=0, keepdims=True)


def range_top_kernel(core_ref, mine_ref, other_ref, share_ref, gram_ref, top_ref, rows_ref):
    gram = whole_of(core_ref, mine_ref[...], other_ref[...])
    gram_ref[...] = gram
    h = top_ref.shape[0]
    top = chol_inverse(gram[:h, :h], 8)
    top_ref[...] = top
    rows_ref[...] = exact(top, share_ref[:h, :])


def rest_of_basis(gram_rows, top_gram, top, top_rows, share, out_ref, scale):
    h = top.shape[0]
    side = exact(gram_rows[:, :h], top, 1, 1)
    rest = gram_rows[:, h:] - exact(side, side, 1, 1)
    left = share - exact(side, top_rows)
    out_ref[:, :h] = top_rows.T * scale
    low = chol_inverse(rest, 8)
    out_ref[:, h:] = exact(left, low, 0, 1) * scale
    corner = exact(exact(low, side), top)
    first, second = diagonal_of(top_gram), diagonal_of(gram_rows[:, h:])
    squares = (top * top + corner * corner) * first + low * low * second
    return check_of(squares, (first, second))


def range_rest_kernel(gram_ref, top_ref, rows_ref, share_ref, out_ref, check_ref, *, scale):
    h = top_ref.shape[0]
    check_ref[...] = rest_of_basis(
        gram_ref[h:, :], gram_ref[:h, :h], top_ref[...], rows_ref[...], share_ref[h:, :], out_ref, scale
    )


def basis_kernel(core_ref, mine_ref, other_ref, share_ref, before_ref, out_ref, check_ref, *, scale):
    gram = whole_of(core_ref, mine_ref[...], other_ref[...])
    h = gram.shape[0] // 2
    top = chol_inverse(gram[:h, :h], 8)
    rows = exact(top, share_ref[:h, :])
    check = rest_of_basis(gram[h:, :], gram[:h, :h], top, rows, share_ref[h:, :], out_ref, scale)
    check_ref[...] = check * before_ref[...]


def tie(value, tokens):
    return lax.optimization_barrier((value, *tokens))[0] if tokens else value


def swap(value, axis, bit):
    n = lax.axis_size(axis)
    return lax.ppermute(value, axis, [(i, i ^ bit) for i in range(n)])


def bits_of(n, first):
    bits = []
    bit = first
    while bit < n:
        bits.append(bit)
        bit *= 2
    return bits


def sum_over_chips(order, keep, give):
    pairs, k, share = keep.shape
    bits = bits_of(lax.axis_size("col"), 2)
    message = jax.ShapeDtypeStruct((k // 2, pairs * share + 128), jnp.int16)
    received = swap(give, "col", 1)
    yield
    halves = order.run(code_first_kernel, [message, message], (keep, received), (IN_VMEM,) * 2, "code_cores")
    for level in range(len(bits)):
        moved = [swap(v, "col", bits[(level + t) % len(bits)]) for t, v in enumerate(halves)]
        yield
        operands = (halves[0], moved[0], halves[1], moved[1])
        if level < len(bits) - 1:
            halves = order.run(
                functools.partial(code_next_kernel, pairs=pairs, share=share),
                [message, message],
                operands,
                (IN_VMEM,) * 4,
                "code_chips",
            )
        else:
            (total,) = order.run(
                code_last_kernel, [jax.ShapeDtypeStruct(keep.shape, F32)], operands, (IN_VMEM,) * 4, "sum_chips"
            )
    return total


def sum_over_rows(order, half):
    for bit in bits_of(lax.axis_size("row"), 1):
        other = swap(half, "row", bit)
        yield
        (half,) = order.run(
            functools.partial(add_kernel, n=1),
            [jax.ShapeDtypeStruct(half.shape, F32)],
            (half, other),
            (IN_VMEM,) * 2,
            "sum_rows",
        )
    return half, swap(half, "col", 1)


def keep_and_give(order, core, gram):
    half = jax.ShapeDtypeStruct((gram.shape[0] // 2, gram.shape[1]), F32)
    return order.run(keep_give_kernel, [half, half], (core, gram), (IN_SMEM, IN_VMEM), "gram_halves")


def sum_over_all(order, core, gram):
    keep, give = keep_and_give(order, core, gram)
    received = swap(give, "col", 1)
    yield
    (half,) = order.run(
        functools.partial(add_kernel, n=1),
        [jax.ShapeDtypeStruct(keep.shape, F32)],
        (keep, received),
        (IN_VMEM,) * 2,
        "sum_gram_cores",
    )
    half, other = yield from sum_over_rows(order, half)
    yield
    return half, other


class Jobs:
    def __init__(self):
        self.active = []

    def add(self, steps):
        self.active.append(steps)
        return self.advance(steps)

    def advance(self, steps):
        try:
            next(steps)
        except StopIteration:
            self.active.remove(steps)

    def step(self):
        for steps in list(self.active):
            self.advance(steps)

    def finish(self):
        while self.active:
            self.step()


def scan_rows(order, jobs, splits, done, last, slab, core, k, pairs, share):
    n = lax.axis_size("row")
    roles = n // 2
    i = lax.axis_index("row")
    even = (i % 2) == 0
    hop_even = jnp.where(even, i, n - 1 - i)
    hop_odd = jnp.where(even, n - 1 - i, i)
    role_even = (hop_even // 2).astype(jnp.int32)[None]
    role_odd = jnp.minimum((hop_odd - 1) // 2, max(roles - 2, 0)).astype(jnp.int32)[None]
    role_sum = (jnp.where(even, n - 2 - i, i - 1) // 2).astype(jnp.int32)[None]
    pairs_even = [(j, j ^ 1) for j in range(n)]
    pairs_odd = [(j, j + 1) for j in range(1, n - 1, 2)] + [(j + 1, j) for j in range(1, n - 1, 2)]
    chunks = len(done)
    per = len(slab)
    height, piece = slab[0].shape
    m = chunks * per
    own = {}

    def own_of(q):
        q = min(max(q, 0), m - 1)
        if q not in own:
            while q // per not in splits:
                jobs.step()
            (own[q],) = order.run(
                cross_kernel,
                [jax.ShapeDtypeStruct((k, piece), F32)],
                (splits[q // per], slab[q % per]),
                (IN_VMEM, IN_VMEM),
                "cross_piece",
            )
        return own[q]

    sent_even, sent_odd = {}, {}
    n_even = m + (roles - 1) * LAG
    n_odd = m + (roles - 2) * LAG if roles > 1 else 0
    message = [jax.ShapeDtypeStruct((k, piece), BF16)]

    def send_even(s):
        if s >= n_even or s in sent_even:
            return
        owns = [own_of(s - role * LAG) for role in range(roles)]
        received = sent_odd.get(s - LAG)
        operands = (role_even, *owns) + ((received,) if received is not None else ())
        (value,) = order.run(
            functools.partial(pick_kernel, n=roles, has_received=received is not None),
            message,
            operands,
            (IN_SMEM,) + (IN_VMEM,) * (len(operands) - 1),
            "send_even",
        )
        sent_even[s] = lax.ppermute(value, "row", pairs_even)

    def send_odd(s):
        if not 0 <= s < n_odd:
            return
        owns = [own_of(s - role * LAG) for role in range(roles - 1)]
        (value,) = order.run(
            functools.partial(send_on_kernel, n=roles - 1),
            message,
            (role_odd, *owns, sent_even[s]),
            (IN_SMEM,) + (IN_VMEM,) * roles,
            "send_odd",
        )
        sent_odd[s] = lax.ppermute(value, "row", pairs_odd)

    seconds = [None] * chunks
    nothing = jnp.zeros((k, piece), BF16)

    def odd_for(q, role):
        hop = n - 3 - 2 * role
        return nothing if hop < 0 else sent_odd[q + ((hop - 1) // 2) * LAG]

    def product(q):
        if not 0 <= q < m:
            return
        evens = [sent_even[q + role * LAG] for role in range(roles)]
        odds = [odd_for(q, role) for role in range(roles)]
        base = seconds[q // per]
        has_base = base is not None
        operands = (core, role_sum, own_of(q), slab[q % per], *evens, *odds, *(base or ()))
        seconds[q // per] = order.run(
            functools.partial(second_kernel, n=roles, has_base=has_base),
            [jax.ShapeDtypeStruct((pairs, k, share), F32)] * 2,
            operands,
            (IN_SMEM, IN_SMEM) + (IN_VMEM,) * (len(operands) - 2),
            "second_piece",
            scratch=(pltpu.VMEM((2 * k, piece), BF16),),
            aliases={len(operands) - 2: 0, len(operands) - 1: 1} if has_base else None,
        )
        if q % per == per - 1:
            done[q // per](*seconds[q // per])

    send_even(0)
    for s in range(n_even):
        need = s + 1 - LAG
        if need < 0 or need in sent_odd or need >= n_odd:
            send_even(s + 1)
        send_odd(s)
        send_even(s + 1)
        if s == max(n_even - 3, 0):
            last()
        jobs.step()
        product(s - (roles - 1) * LAG)


def body(tile_data, tile_rows, tile_cols, tile_count, sketch):
    tiles = tile_data[0, 0]
    row_index = tile_rows[0, 0]
    col_index = tile_cols[0, 0]
    count = tile_count[0]
    edge = tiles.shape[1]
    k = sketch.shape[1]
    height, width = RB_G * edge, CB_G * edge
    shares = lax.axis_size("col")
    pairs = shares // 2
    share = height // shares
    scale = math.sqrt(height * lax.axis_size("row"))
    me = lax.axis_index("col")
    core = (me % 2).astype(jnp.int32)[None]
    order, jobs = Order(), Jobs()

    part = jax.ShapeDtypeStruct((pairs, k, share), F32)
    piece = width // PIECES
    slab_and_parts = pl.pallas_call(
        functools.partial(dense_first_kernel, chunks=CHUNKS, pieces=PIECES),
        out_shape=[pltpu.HBM((height, piece), BF16)] * PIECES + [part] * (2 * CHUNKS),
        in_specs=[IN_SMEM] * 4 + [ANYWHERE, IN_VMEM],
        out_specs=[IN_HBM] * PIECES + [IN_VMEM] * (2 * CHUNKS),
        scratch_shapes=[
            pltpu.VMEM((PIECES, height, piece), BF16),
            pltpu.VMEM((k, width), BF16),
            pltpu.SemaphoreType.DMA,
            pltpu.SemaphoreType.DMA((PIECES,)),
        ],
        compiler_params=pltpu.CompilerParams(vmem_limit_bytes=24 * MIB),
        cost_estimate=SMALL,
        name="dense_first",
    )(core, row_index, col_index, count, tiles, sketch)
    slab, parts = slab_and_parts[:PIECES], slab_and_parts[PIECES:]

    def own_rows(blocks):
        return lax.dynamic_index_in_dim(blocks, me // 2, 0, keepdims=False)

    ready = jax.ShapeDtypeStruct((8, 128), F32)
    out = jax.ShapeDtypeStruct((share, k), F32)
    whole = jax.ShapeDtypeStruct((k, k), F32)
    h = k // 2
    first, splits, result = [], {}, {}

    def first_sum():
        total = yield from sum_over_chips(order, *parts)
        other = swap(total, "col", 1)
        yield
        first.extend((total, other))
        (splits[0],) = order.run(
            split_kernel,
            [jax.ShapeDtypeStruct((2 * k, height), BF16)],
            (core, total, other),
            (IN_SMEM, IN_VMEM, IN_VMEM),
            "split",
        )

    def range_one():
        yield
        yield
        yield
        (gram,) = order.run(
            functools.partial(gram_one_kernel, chunks=1), [whole], first, (IN_VMEM,) * 2, "gram_one"
        )
        keep, _ = keep_and_give(order, core, gram)
        while "last" not in result:
            yield
        half, other = yield from sum_over_rows(order, keep)
        rows = own_rows(first[0])
        yield
        gram, top, top_rows = order.run(
            range_top_kernel,
            [whole, jax.ShapeDtypeStruct((h, h), F32), jax.ShapeDtypeStruct((h, share), F32)],
            (core, half, other, rows),
            (IN_SMEM,) + (IN_VMEM,) * 3,
            "range_top",
        )
        yield
        result["range"] = order.run(
            functools.partial(range_rest_kernel, scale=scale),
            [out, ready],
            (gram, top, top_rows, rows),
            (IN_VMEM,) * 4,
            "range_rest",
        )

    def basis_of(keep, give):
        total = yield from sum_over_chips(order, keep, give)
        (gram,) = order.run(functools.partial(gram_kernel, n=1), [whole], (total,), (IN_VMEM,), "gram_two")
        half, other = yield from sum_over_all(order, core, gram)
        while "range" not in result:
            yield
        result["basis"] = order.run(
            functools.partial(basis_kernel, scale=scale),
            [out, ready],
            (core, half, other, own_rows(total), result["range"][1]),
            (IN_SMEM,) + (IN_VMEM,) * 4,
            "basis",
        )

    def finished(keep, give):
        steps = basis_of(keep, give)
        jobs.active.insert(0, steps)
        jobs.advance(steps)

    jobs.add(first_sum())
    jobs.finish()
    jobs.add(range_one())
    scan_rows(order, jobs, splits, [finished], lambda: result.update(last=True), slab, core, k, pairs, share)
    jobs.finish()
    range_out = result["range"][0]
    basis, check = result["basis"]
    return lax.cond(
        check[0, 0] > 0.5,
        lambda: (range_out, basis),
        lambda: plain_way(tiles, row_index, col_index, tile_count[0, 0], sketch),
    )


def solution(mesh):
    placed = (
        P("row", "col", None, None, None),
        P("row", "col", None),
        P("row", "col", None),
        P("row", "col"),
        P("col", None),
    )
    return jax.shard_map(
        body,
        mesh=mesh,
        in_specs=placed,
        out_specs=(P(("row", "col"), None), P(("row", "col"), None)),
        check_vma=False,
    )
```

```python
import functools
import math

import jax
import jax.numpy as jnp
from jax import lax
from jax.experimental import pallas as pl
from jax.experimental.pallas import tpu as pltpu
from jax.sharding import PartitionSpec as P

RB_G = 16
CB_G = 32
CHUNKS = 1
PIECES = 8
LAG = 3
CODE_MAX = 32700.0
GAIN_MAX = 6.0
DIAG_MIN = 1e-24
DIAG_MAX = 1e30
F32 = jnp.float32
BF16 = jnp.bfloat16
MIB = 1024 * 1024
SMALL = pl.CostEstimate(flops=1, bytes_accessed=1, transcendentals=0)
IN_VMEM = pl.BlockSpec(memory_space=pltpu.VMEM)
IN_SMEM = pl.BlockSpec(memory_space=pltpu.SMEM)
ANYWHERE = pl.BlockSpec(memory_space=pl.ANY)
IN_HBM = pl.BlockSpec(memory_space=pltpu.HBM)


def tile_product(tiles, out_index, in_index, count, operand, n_out, flip):
    total_tiles = tiles.shape[0]
    width = min(64, total_tiles)
    blocks = total_tiles // width
    form = "tba,tbk->tak" if flip else "tab,tbk->tak"
    targets = jnp.arange(n_out, dtype=jnp.int32)

    def step(number, total):
        start = number * width
        block = lax.dynamic_slice_in_dim(tiles, start, width, 0)
        target = lax.dynamic_slice_in_dim(out_index, start, width, 0)
        source = lax.dynamic_slice_in_dim(in_index, start, width, 0)
        gathered = jnp.take(operand, source, axis=0)
        product = jnp.einsum(form, block, gathered, preferred_element_type=F32)
        weight = (start + jnp.arange(width, dtype=jnp.int32) < count).astype(F32)
        select = (target[None, :] == targets[:, None]).astype(F32) * weight[None, :]
        return total + jnp.einsum("nt,tak->nak", select, product, precision=lax.Precision.HIGHEST)

    start_total = jnp.zeros((n_out, tiles.shape[1], operand.shape[2]), F32)
    return lax.fori_loop(0, blocks, step, start_total)


def gram_of(values):
    return jnp.dot(values.T, values, precision=lax.Precision.HIGHEST)


def orthonormal(values, gram):
    lower = jnp.linalg.cholesky(gram)
    inverse = lax.linalg.triangular_solve(
        lower, jnp.eye(gram.shape[0], dtype=F32), left_side=True, lower=True
    )
    return jnp.dot(values, inverse.T, precision=lax.Precision.HIGHEST)


def sum_over(value, axis):
    n = lax.axis_size(axis)
    if n & (n - 1):
        return lax.psum(value, axis)
    bit = 1
    while bit < n:
        value = value + lax.ppermute(value, axis, [(i, i ^ bit) for i in range(n)])
        bit *= 2
    return value


def plain_way(tiles, row_index, col_index, count, sketch):
    edge = tiles.shape[1]
    width_k = sketch.shape[1]
    scale_rows = math.sqrt(RB_G * edge * lax.axis_size("row"))
    omega = sketch.reshape(CB_G, edge, width_k)
    first = tile_product(tiles, row_index, col_index, count, omega, RB_G, False)
    first = first.reshape(RB_G * edge, width_k)
    whole = sum_over(first, "col")
    gram = sum_over(gram_of(whole), "row")
    whole_float = orthonormal(whole, gram)
    share_rows = whole.shape[0] // lax.axis_size("col")
    mine = lax.dynamic_slice_in_dim(whole_float, lax.axis_index("col") * share_rows, share_rows, 0)
    ortho_one = whole_float.astype(BF16).reshape(RB_G, edge, width_k)
    cross = tile_product(tiles, col_index, row_index, count, ortho_one, CB_G, True)
    cross = cross.reshape(CB_G * edge, width_k)
    cross_full = sum_over(cross, "row").astype(BF16).reshape(CB_G, edge, width_k)
    second = tile_product(tiles, row_index, col_index, count, cross_full, RB_G, False)
    second = second.reshape(RB_G * edge, width_k)
    second = sum_over(second, "col")
    second_share = lax.dynamic_slice_in_dim(second, lax.axis_index("col") * share_rows, share_rows, 0)
    gram_two = sum_over(gram_of(second), "row")
    return mine * scale_rows, orthonormal(second_share, gram_two) * scale_rows


class Order:
    def __init__(self):
        self.token = None

    def run(self, kernel, outs, operands, specs, name, limit=12, scratch=(), aliases=None):
        n_in, n_out = len(operands), len(outs)
        tokens = () if self.token is None else (self.token,)

        def ordered(*refs):
            results = refs[n_in + len(tokens) :]
            results[n_out][...] = jnp.zeros(results[n_out].shape, F32)
            kernel(*refs[:n_in], *results[:n_out], *results[n_out + 1 :])

        *results, self.token = pl.pallas_call(
            ordered,
            out_shape=[*outs, jax.ShapeDtypeStruct((8, 128), F32)],
            in_specs=list(specs) + [ANYWHERE] * len(tokens),
            out_specs=[IN_VMEM] * (n_out + 1),
            scratch_shapes=list(scratch),
            input_output_aliases=aliases or {},
            compiler_params=pltpu.CompilerParams(vmem_limit_bytes=limit * MIB),
            cost_estimate=SMALL,
            name=name,
        )(*operands, *tokens)
        return results


def exact(a, b, ca=1, cb=0):
    return lax.dot_general(
        a, b, (((ca,), (cb,)), ((), ())), precision=lax.Precision.HIGHEST, preferred_element_type=F32
    )


def dense_first_kernel(
    core_ref, rows_ref, cols_ref, count_ref, tiles_ref, sketch_ref, *refs, chunks, pieces
):
    slabs, outs = refs[:pieces], refs[pieces : pieces + 2 * chunks]
    slab_ref, turned_ref, sem, out_sems = refs[pieces + 2 * chunks :]
    _, height, piece = slab_ref.shape
    edge = tiles_ref.shape[1]
    per = piece // edge

    def clear(i, carry):
        for p in range(pieces):
            slab_ref[p, pl.ds(pl.multiple_of(i * edge, edge), edge), :] = jnp.zeros((edge, piece), slab_ref.dtype)
        return carry

    lax.fori_loop(0, height // edge, clear, 0)
    count = count_ref[0]

    def place(t):
        r = pl.multiple_of(rows_ref[t] * edge, edge)
        c = cols_ref[t]
        at = pl.multiple_of(lax.rem(c, per) * edge, edge)
        return pltpu.make_async_copy(
            tiles_ref.at[t], slab_ref.at[lax.div(c, per), pl.ds(r, edge), pl.ds(at, edge)], sem
        )

    def start(t, carry):
        place(t).start()
        return carry

    def start_four(i, carry):
        for j in range(4):
            place(4 * i + j).start()
        return carry

    lax.fori_loop(0, lax.div(count, 4), start_four, 0)
    lax.fori_loop(4 * lax.div(count, 4), count, start, 0)
    for j in range(pieces * per):
        turned_ref[:, j * edge : (j + 1) * edge] = sketch_ref[j * edge : (j + 1) * edge, :].T
    bit = 1
    while bit <= tiles_ref.shape[0]:

        @pl.when(lax.rem(lax.div(count, bit), 2) == 1)
        def _(bit=bit):
            some = tiles_ref.at[pl.ds(0, bit)]
            pltpu.make_async_copy(some, some, sem).wait()

        bit *= 2
    writes = [
        pltpu.make_async_copy(slab_ref.at[p], slabs[p], out_sems.at[p]) for p in range(pieces)
    ]
    for write in writes:
        write.start()
    core = core_ref[0]
    pairs, k, share = outs[0].shape

    def step(j, carry):
        for side in range(2):
            i = 2 * j + (core if side == 0 else 1 - core)
            at = pl.ds(pl.multiple_of(i * share, share), share)
            value = None
            for p in range(pieces):
                block = slab_ref[p, at, :]
                term = lax.dot_general(
                    turned_ref[:, p * piece : (p + 1) * piece],
                    block,
                    (((1,), (1,)), ((), ())),
                    preferred_element_type=F32,
                )
                value = term if value is None else value + term
            for c in range(chunks):
                outs[2 * c + side][j] = value[c * k : (c + 1) * k]
        return carry

    lax.fori_loop(0, pairs, step, 0)
    for write in writes:
        write.wait()


def split_kernel(core_ref, mine_ref, other_ref, out_ref):
    pairs, k, share = mine_ref.shape
    core = core_ref[0]
    for i in range(pairs):
        for parity, ref in ((core, mine_ref), (1 - core, other_ref)):
            value = ref[i]
            high = value.astype(BF16)
            at = pl.ds(pl.multiple_of((2 * i + parity) * share, share), share)
            out_ref[:k, at] = high
            out_ref[k:, at] = (value - high.astype(F32)).astype(BF16)


def gram_one_kernel(*refs, chunks):
    out_ref = refs[-1]

    def of(lists, i):
        rows = jnp.concatenate([ref[i] for ref in lists], axis=0)
        return exact(rows, rows, 1, 1)

    out_ref[...] = jnp.zeros(out_ref.shape, F32)

    def step(i, carry):
        out_ref[...] += of(refs[:chunks], i) + of(refs[chunks : 2 * chunks], i)
        return carry

    lax.fori_loop(0, refs[0].shape[0], step, 0)


def gram_kernel(*refs, n):
    out_ref = refs[-1]
    k = out_ref.shape[0]
    out_ref[...] = jnp.zeros(out_ref.shape, F32)

    def step(i, carry):
        rows = jnp.concatenate([ref[i] for ref in refs[:n]], axis=0)
        out_ref[...] += exact(rows[(n - 1) * k :], rows, 1, 1)
        return carry

    lax.fori_loop(0, refs[0].shape[0], step, 0)


def cross_kernel(split_ref, slab_ref, out_ref):
    k, width = out_ref.shape
    step = min(512, width)

    def part(i, carry):
        at = pl.ds(pl.multiple_of(i * step, step), step)
        both = jnp.dot(split_ref[...], slab_ref[:, at], preferred_element_type=F32)
        out_ref[:, at] = both[:k] + both[k:]
        return carry

    lax.fori_loop(0, width // step, part, 0)


def pick_kernel(role_ref, *refs, n, has_received):
    received = refs[n] if has_received else None
    out_ref = refs[-1]
    for role in range(n):

        @pl.when(role_ref[0] == role)
        def _(role=role):
            value = refs[role][...]
            if has_received and role > 0:
                value = value + received[...].astype(F32)
            out_ref[...] = value.astype(out_ref.dtype)


def send_on_kernel(role_ref, *refs, n):
    for role in range(n):

        @pl.when(role_ref[0] == role)
        def _(role=role):
            refs[-1][...] = (refs[role][...] + refs[n][...].astype(F32)).astype(refs[-1].dtype)


def second_kernel(core_ref, role_ref, own_ref, slab_ref, *refs, n, has_base):
    even_refs, odd_refs = refs[:n], refs[n : 2 * n]
    bases = refs[2 * n : 2 * n + 2] if has_base else (None, None)
    at = 2 * n + 2 * has_base
    outs, total_ref = refs[at : at + 2], refs[at + 2]
    k = own_ref.shape[0]
    pairs, _, share = outs[0].shape
    core = core_ref[0]
    for role in range(n):

        @pl.when(role_ref[0] == role)
        def _(role=role):
            total = own_ref[...] + even_refs[role][...].astype(F32) + odd_refs[role][...].astype(F32)
            high = total.astype(BF16)
            total_ref[:k, :] = high
            total_ref[k:, :] = (total - high.astype(F32)).astype(BF16)

    def step(j, carry):
        for side in range(2):
            i = 2 * j + (core if side == 0 else 1 - core)
            block = slab_ref[pl.ds(pl.multiple_of(i * share, share), share), :]
            both = lax.dot_general(
                total_ref[...], block, (((1,), (1,)), ((), ())), preferred_element_type=F32
            )
            value = both[:k] + both[k:]
            outs[side][j] = bases[side][j] + value if has_base else value
        return carry

    lax.fori_loop(0, pairs, step, 0, unroll=2)


def add_kernel(*refs, n):
    for i in range(n):
        refs[2 * n + i][...] = refs[2 * i][...] + refs[2 * i + 1][...]


def encode(blocks, low_ref, high_ref):
    h = low_ref.shape[0]
    share = blocks[0].shape[1]
    most = functools.reduce(jnp.maximum, [jnp.max(jnp.abs(v), axis=1, keepdims=True) for v in blocks])
    power = jnp.ceil(jnp.log2(jnp.maximum(most, 1e-36) * (1.0 / CODE_MAX)))
    inverse = jnp.exp2(-power)
    for i, v in enumerate(blocks):
        code = jnp.round(v * inverse).astype(jnp.int32).astype(jnp.int16)
        at = slice(i * share, (i + 1) * share)
        low_ref[:, at] = code[:h]
        high_ref[:, at] = code[h:]
    tail = slice(len(blocks) * share, low_ref.shape[1])
    width = low_ref.shape[1] - len(blocks) * share
    power = jnp.broadcast_to(power, (2 * h, width)).astype(jnp.int32).astype(jnp.int16)
    low_ref[:, tail] = power[:h]
    high_ref[:, tail] = power[h:]


def decode(ref, pairs, share):
    power = ref[:, pairs * share : pairs * share + 128].astype(jnp.int32).astype(F32)
    factor = jnp.exp2(jnp.max(power, axis=1, keepdims=True))
    return [
        ref[:, i * share : (i + 1) * share].astype(jnp.int32).astype(F32) * factor for i in range(pairs)
    ]


def code_first_kernel(a_ref, b_ref, low_ref, high_ref):
    encode([a_ref[i] + b_ref[i] for i in range(a_ref.shape[0])], low_ref, high_ref)


def decoded_sums(refs, pairs, share):
    low, low_more, high, high_more = [decode(ref, pairs, share) for ref in refs]
    return [
        jnp.concatenate([low[i] + low_more[i], high[i] + high_more[i]], axis=0) for i in range(pairs)
    ]


def code_next_kernel(*refs, pairs, share):
    encode(decoded_sums(refs[:4], pairs, share), refs[4], refs[5])


def code_last_kernel(*refs):
    out_ref = refs[4]
    for i, v in enumerate(decoded_sums(refs[:4], out_ref.shape[0], out_ref.shape[2])):
        out_ref[i] = v


def keep_give_kernel(core_ref, value_ref, keep_ref, give_ref):
    h = keep_ref.shape[0]
    core = core_ref[0]
    keep_ref[...] = value_ref[pl.ds(pl.multiple_of(core * h, h), h), :]
    give_ref[...] = value_ref[pl.ds(pl.multiple_of((1 - core) * h, h), h), :]


def whole_of(core_ref, mine, other):
    core = core_ref[0] == 0
    return jnp.concatenate([jnp.where(core, mine, other), jnp.where(core, other, mine)], axis=0)


def chol_inverse(a, step):
    n = a.shape[0]
    rows = lax.broadcasted_iota(jnp.int32, (n, n), 0)
    lanes = lax.broadcasted_iota(jnp.int32, (n, n), 1)
    lane = lax.broadcasted_iota(jnp.int32, (1, n), 1)
    pivots = jnp.ones((1, n), F32)
    done = []
    for k in range(0, n, step):
        m = a.shape[0]
        cols = [jnp.broadcast_to(a[:, k + j : k + j + 1], (m, n)) for j in range(step)]
        s = [[cols[q][j : j + 1, :] for q in range(step)] for j in range(step)]
        r = [a[j : j + 1, :] for j in range(step)]
        update = None
        for j in range(step):
            inverse = 1.0 / s[j][j]
            pivots = jnp.where(lane == k + j, s[j][j], pivots)
            row = r[j] + jnp.where(lane == k + j, s[j][j], 0.0)
            for q in range(j + 1, step):
                factor = s[q][j] * inverse
                r[q] = r[q] - factor * row
                for p in range(j + 1, step):
                    s[q][p] = s[q][p] - factor * s[j][p]
            column = cols[j] * inverse
            for q in range(j + 1, step):
                cols[q] = cols[q] - column * s[j][q]
            update = column * row if update is None else update + column * row
        done.extend(r)
        if m > step:
            a = a[step:] - update[step:]
    full = jnp.concatenate(done, 0)
    root = jnp.broadcast_to(lax.rsqrt(pivots), (n, n))
    by_row = jnp.sum(jnp.where(rows == lanes, root, 0.0), axis=1, keepdims=True)
    return jnp.where(lanes <= rows, full * (1.0 / pivots) * by_row, 0.0)


def check_of(squares, diagonals):
    k = sum(d.shape[1] for d in diagonals)
    gain = jnp.sum(jnp.sum(squares, axis=1, keepdims=True), axis=0, keepdims=True) / k
    good = gain < GAIN_MAX
    for diagonal in diagonals:
        good &= (jnp.min(diagonal, axis=1, keepdims=True) > DIAG_MIN) & (
            jnp.max(diagonal, axis=1, keepdims=True) < DIAG_MAX
        )
    return jnp.broadcast_to(jnp.where(good, 1.0, 0.0), (8, 128))


def diagonal_of(gram):
    k = gram.shape[0]
    rows = lax.broadcasted_iota(jnp.int32, (k, k), 0)
    lanes = lax.broadcasted_iota(jnp.int32, (k, k), 1)
    return jnp.sum(jnp.where(rows == lanes, gram, 0.0), axis=0, keepdims=True)


def range_top_kernel(core_ref, mine_ref, other_ref, share_ref, gram_ref, top_ref, rows_ref):
    gram = whole_of(core_ref, mine_ref[...], other_ref[...])
    gram_ref[...] = gram
    h = top_ref.shape[0]
    top = chol_inverse(gram[:h, :h], 8)
    top_ref[...] = top
    rows_ref[...] = exact(top, share_ref[:h, :])


def rest_of_basis(gram_rows, top_gram, top, top_rows, share, out_ref, scale):
    h = top.shape[0]
    side = exact(gram_rows[:, :h], top, 1, 1)
    rest = gram_rows[:, h:] - exact(side, side, 1, 1)
    left = share - exact(side, top_rows)
    out_ref[:, :h] = top_rows.T * scale
    low = chol_inverse(rest, 8)
    out_ref[:, h:] = exact(left, low, 0, 1) * scale
    corner = exact(exact(low, side), top)
    first, second = diagonal_of(top_gram), diagonal_of(gram_rows[:, h:])
    squares = (top * top + corner * corner) * first + low * low * second
    return check_of(squares, (first, second))


def range_rest_kernel(gram_ref, top_ref, rows_ref, share_ref, out_ref, check_ref, *, scale):
    h = top_ref.shape[0]
    check_ref[...] = rest_of_basis(
        gram_ref[h:, :], gram_ref[:h, :h], top_ref[...], rows_ref[...], share_ref[h:, :], out_ref, scale
    )


def basis_kernel(core_ref, mine_ref, other_ref, share_ref, before_ref, out_ref, check_ref, *, scale):
    gram = whole_of(core_ref, mine_ref[...], other_ref[...])
    h = gram.shape[0] // 2
    top = chol_inverse(gram[:h, :h], 8)
    rows = exact(top, share_ref[:h, :])
    check = rest_of_basis(gram[h:, :], gram[:h, :h], top, rows, share_ref[h:, :], out_ref, scale)
    check_ref[...] = check * before_ref[...]


def tie(value, tokens):
    return lax.optimization_barrier((value, *tokens))[0] if tokens else value


def swap(value, axis, bit):
    n = lax.axis_size(axis)
    return lax.ppermute(value, axis, [(i, i ^ bit) for i in range(n)])


def bits_of(n, first):
    bits = []
    bit = first
    while bit < n:
        bits.append(bit)
        bit *= 2
    return bits


def sum_over_chips(order, keep, give):
    pairs, k, share = keep.shape
    bits = bits_of(lax.axis_size("col"), 2)
    message = jax.ShapeDtypeStruct((k // 2, pairs * share + 128), jnp.int16)
    received = swap(give, "col", 1)
    yield
    halves = order.run(code_first_kernel, [message, message], (keep, received), (IN_VMEM,) * 2, "code_cores")
    for level in range(len(bits)):
        moved = [swap(v, "col", bits[(level + t) % len(bits)]) for t, v in enumerate(halves)]
        yield
        operands = (halves[0], moved[0], halves[1], moved[1])
        if level < len(bits) - 1:
            halves = order.run(
                functools.partial(code_next_kernel, pairs=pairs, share=share),
                [message, message],
                operands,
                (IN_VMEM,) * 4,
                "code_chips",
            )
        else:
            (total,) = order.run(
                code_last_kernel, [jax.ShapeDtypeStruct(keep.shape, F32)], operands, (IN_VMEM,) * 4, "sum_chips"
            )
    return total


def sum_over_rows(order, half):
    for bit in bits_of(lax.axis_size("row"), 1):
        other = swap(half, "row", bit)
        yield
        (half,) = order.run(
            functools.partial(add_kernel, n=1),
            [jax.ShapeDtypeStruct(half.shape, F32)],
            (half, other),
            (IN_VMEM,) * 2,
            "sum_rows",
        )
    return half, swap(half, "col", 1)


def keep_and_give(order, core, gram):
    half = jax.ShapeDtypeStruct((gram.shape[0] // 2, gram.shape[1]), F32)
    return order.run(keep_give_kernel, [half, half], (core, gram), (IN_SMEM, IN_VMEM), "gram_halves")


def sum_over_all(order, core, gram):
    keep, give = keep_and_give(order, core, gram)
    received = swap(give, "col", 1)
    yield
    (half,) = order.run(
        functools.partial(add_kernel, n=1),
        [jax.ShapeDtypeStruct(keep.shape, F32)],
        (keep, received),
        (IN_VMEM,) * 2,
        "sum_gram_cores",
    )
    half, other = yield from sum_over_rows(order, half)
    yield
    return half, other


class Jobs:
    def __init__(self):
        self.active = []

    def add(self, steps):
        self.active.append(steps)
        return self.advance(steps)

    def advance(self, steps):
        try:
            next(steps)
        except StopIteration:
            self.active.remove(steps)

    def step(self):
        for steps in list(self.active):
            self.advance(steps)

    def finish(self):
        while self.active:
            self.step()


def scan_rows(order, jobs, splits, done, last, slab, core, k, pairs, share):
    n = lax.axis_size("row")
    roles = n // 2
    i = lax.axis_index("row")
    even = (i % 2) == 0
    hop_even = jnp.where(even, i, n - 1 - i)
    hop_odd = jnp.where(even, n - 1 - i, i)
    role_even = (hop_even // 2).astype(jnp.int32)[None]
    role_odd = jnp.minimum((hop_odd - 1) // 2, max(roles - 2, 0)).astype(jnp.int32)[None]
    role_sum = (jnp.where(even, n - 2 - i, i - 1) // 2).astype(jnp.int32)[None]
    pairs_even = [(j, j ^ 1) for j in range(n)]
    pairs_odd = [(j, j + 1) for j in range(1, n - 1, 2)] + [(j + 1, j) for j in range(1, n - 1, 2)]
    chunks = len(done)
    per = len(slab)
    height, piece = slab[0].shape
    m = chunks * per
    own = {}

    def own_of(q):
        q = min(max(q, 0), m - 1)
        if q not in own:
            while q // per not in splits:
                jobs.step()
            (own[q],) = order.run(
                cross_kernel,
                [jax.ShapeDtypeStruct((k, piece), F32)],
                (splits[q // per], slab[q % per]),
                (IN_VMEM, IN_VMEM),
                "cross_piece",
            )
        return own[q]

    sent_even, sent_odd = {}, {}
    n_even = m + (roles - 1) * LAG
    n_odd = m + (roles - 2) * LAG if roles > 1 else 0
    message = [jax.ShapeDtypeStruct((k, piece), BF16)]

    def send_even(s):
        if s >= n_even or s in sent_even:
            return
        owns = [own_of(s - role * LAG) for role in range(roles)]
        received = sent_odd.get(s - LAG)
        operands = (role_even, *owns) + ((received,) if received is not None else ())
        (value,) = order.run(
            functools.partial(pick_kernel, n=roles, has_received=received is not None),
            message,
            operands,
            (IN_SMEM,) + (IN_VMEM,) * (len(operands) - 1),
            "send_even",
        )
        sent_even[s] = lax.ppermute(value, "row", pairs_even)

    def send_odd(s):
        if not 0 <= s < n_odd:
            return
        owns = [own_of(s - role * LAG) for role in range(roles - 1)]
        (value,) = order.run(
            functools.partial(send_on_kernel, n=roles - 1),
            message,
            (role_odd, *owns, sent_even[s]),
            (IN_SMEM,) + (IN_VMEM,) * roles,
            "send_odd",
        )
        sent_odd[s] = lax.ppermute(value, "row", pairs_odd)

    seconds = [None] * chunks
    nothing = jnp.zeros((k, piece), BF16)

    def odd_for(q, role):
        hop = n - 3 - 2 * role
        return nothing if hop < 0 else sent_odd[q + ((hop - 1) // 2) * LAG]

    def product(q):
        if not 0 <= q < m:
            return
        evens = [sent_even[q + role * LAG] for role in range(roles)]
        odds = [odd_for(q, role) for role in range(roles)]
        base = seconds[q // per]
        has_base = base is not None
        operands = (core, role_sum, own_of(q), slab[q % per], *evens, *odds, *(base or ()))
        seconds[q // per] = order.run(
            functools.partial(second_kernel, n=roles, has_base=has_base),
            [jax.ShapeDtypeStruct((pairs, k, share), F32)] * 2,
            operands,
            (IN_SMEM, IN_SMEM) + (IN_VMEM,) * (len(operands) - 2),
            "second_piece",
            scratch=(pltpu.VMEM((2 * k, piece), BF16),),
            aliases={len(operands) - 2: 0, len(operands) - 1: 1} if has_base else None,
        )
        if q % per == per - 1:
            done[q // per](*seconds[q // per])

    send_even(0)
    for s in range(n_even):
        need = s + 1 - LAG
        if need < 0 or need in sent_odd or need >= n_odd:
            send_even(s + 1)
        send_odd(s)
        send_even(s + 1)
        if s == max(n_even - 3, 0):
            last()
        jobs.step()
        product(s - (roles - 1) * LAG)


def body(tile_data, tile_rows, tile_cols, tile_count, sketch):
    tiles = tile_data[0, 0]
    row_index = tile_rows[0, 0]
    col_index = tile_cols[0, 0]
    count = tile_count[0]
    edge = tiles.shape[1]
    k = sketch.shape[1]
    height, width = RB_G * edge, CB_G * edge
    shares = lax.axis_size("col")
    pairs = shares // 2
    share = height // shares
    scale = math.sqrt(height * lax.axis_size("row"))
    me = lax.axis_index("col")
    core = (me % 2).astype(jnp.int32)[None]
    order, jobs = Order(), Jobs()

    part = jax.ShapeDtypeStruct((pairs, k, share), F32)
    piece = width // PIECES
    slab_and_parts = pl.pallas_call(
        functools.partial(dense_first_kernel, chunks=CHUNKS, pieces=PIECES),
        out_shape=[pltpu.HBM((height, piece), BF16)] * PIECES + [part] * (2 * CHUNKS),
        in_specs=[IN_SMEM] * 4 + [ANYWHERE, IN_VMEM],
        out_specs=[IN_HBM] * PIECES + [IN_VMEM] * (2 * CHUNKS),
        scratch_shapes=[
            pltpu.VMEM((PIECES, height, piece), BF16),
            pltpu.VMEM((k, width), BF16),
            pltpu.SemaphoreType.DMA,
            pltpu.SemaphoreType.DMA((PIECES,)),
        ],
        compiler_params=pltpu.CompilerParams(vmem_limit_bytes=24 * MIB),
        cost_estimate=SMALL,
        name="dense_first",
    )(core, row_index, col_index, count, tiles, sketch)
    slab, parts = slab_and_parts[:PIECES], slab_and_parts[PIECES:]

    def own_rows(blocks):
        return lax.dynamic_index_in_dim(blocks, me // 2, 0, keepdims=False)

    ready = jax.ShapeDtypeStruct((8, 128), F32)
    out = jax.ShapeDtypeStruct((share, k), F32)
    whole = jax.ShapeDtypeStruct((k, k), F32)
    h = k // 2
    first, splits, result = [], {}, {}

    def first_sum():
        total = yield from sum_over_chips(order, *parts)
        other = swap(total, "col", 1)
        yield
        first.extend((total, other))
        (splits[0],) = order.run(
            split_kernel,
            [jax.ShapeDtypeStruct((2 * k, height), BF16)],
            (core, total, other),
            (IN_SMEM, IN_VMEM, IN_VMEM),
            "split",
        )

    def range_one():
        yield
        yield
        yield
        (gram,) = order.run(
            functools.partial(gram_one_kernel, chunks=1), [whole], first, (IN_VMEM,) * 2, "gram_one"
        )
        keep, _ = keep_and_give(order, core, gram)
        while "last" not in result:
            yield
        half, other = yield from sum_over_rows(order, keep)
        rows = own_rows(first[0])
        yield
        gram, top, top_rows = order.run(
            range_top_kernel,
            [whole, jax.ShapeDtypeStruct((h, h), F32), jax.ShapeDtypeStruct((h, share), F32)],
            (core, half, other, rows),
            (IN_SMEM,) + (IN_VMEM,) * 3,
            "range_top",
        )
        yield
        result["range"] = order.run(
            functools.partial(range_rest_kernel, scale=scale),
            [out, ready],
            (gram, top, top_rows, rows),
            (IN_VMEM,) * 4,
            "range_rest",
        )

    def basis_of(keep, give):
        total = yield from sum_over_chips(order, keep, give)
        (gram,) = order.run(functools.partial(gram_kernel, n=1), [whole], (total,), (IN_VMEM,), "gram_two")
        half, other = yield from sum_over_all(order, core, gram)
        while "range" not in result:
            yield
        result["basis"] = order.run(
            functools.partial(basis_kernel, scale=scale),
            [out, ready],
            (core, half, other, own_rows(total), result["range"][1]),
            (IN_SMEM,) + (IN_VMEM,) * 4,
            "basis",
        )

    def finished(keep, give):
        steps = basis_of(keep, give)
        jobs.active.insert(0, steps)
        jobs.advance(steps)

    jobs.add(first_sum())
    jobs.finish()
    jobs.add(range_one())
    scan_rows(order, jobs, splits, [finished], lambda: result.update(last=True), slab, core, k, pairs, share)
    jobs.finish()
    range_out = result["range"][0]
    basis, check = result["basis"]
    return lax.cond(
        check[0, 0] > 0.5,
        lambda: (range_out, basis),
        lambda: plain_way(tiles, row_index, col_index, tile_count[0, 0], sketch),
    )


def solution(mesh):
    placed = (
        P("row", "col", None, None, None),
        P("row", "col", None),
        P("row", "col", None),
        P("row", "col"),
        P("col", None),
    )
    return jax.shard_map(
        body,
        mesh=mesh,
        in_specs=placed,
        out_specs=(P(("row", "col"), None), P(("row", "col"), None)),
        check_vma=False,
    )
```

```python
import functools
import math

import jax
import jax.numpy as jnp
from jax import lax
from jax.experimental import pallas as pl
from jax.experimental.pallas import tpu as pltpu
from jax.sharding import PartitionSpec as P

RB_G = 16
CB_G = 32
CHUNKS = 1
PIECES = 8
LAG = 3
CODE_MAX = 32700.0
GAIN_MAX = 6.0
DIAG_MIN = 1e-24
DIAG_MAX = 1e30
F32 = jnp.float32
BF16 = jnp.bfloat16
MIB = 1024 * 1024
SMALL = pl.CostEstimate(flops=1, bytes_accessed=1, transcendentals=0)
IN_VMEM = pl.BlockSpec(memory_space=pltpu.VMEM)
IN_SMEM = pl.BlockSpec(memory_space=pltpu.SMEM)
ANYWHERE = pl.BlockSpec(memory_space=pl.ANY)
IN_HBM = pl.BlockSpec(memory_space=pltpu.HBM)


def tile_product(tiles, out_index, in_index, count, operand, n_out, flip):
    total_tiles = tiles.shape[0]
    width = min(64, total_tiles)
    blocks = total_tiles // width
    form = "tba,tbk->tak" if flip else "tab,tbk->tak"
    targets = jnp.arange(n_out, dtype=jnp.int32)

    def step(number, total):
        start = number * width
        block = lax.dynamic_slice_in_dim(tiles, start, width, 0)
        target = lax.dynamic_slice_in_dim(out_index, start, width, 0)
        source = lax.dynamic_slice_in_dim(in_index, start, width, 0)
        gathered = jnp.take(operand, source, axis=0)
        product = jnp.einsum(form, block, gathered, preferred_element_type=F32)
        weight = (start + jnp.arange(width, dtype=jnp.int32) < count).astype(F32)
        select = (target[None, :] == targets[:, None]).astype(F32) * weight[None, :]
        return total + jnp.einsum("nt,tak->nak", select, product, precision=lax.Precision.HIGHEST)

    start_total = jnp.zeros((n_out, tiles.shape[1], operand.shape[2]), F32)
    return lax.fori_loop(0, blocks, step, start_total)


def gram_of(values):
    return jnp.dot(values.T, values, precision=lax.Precision.HIGHEST)


def orthonormal(values, gram):
    lower = jnp.linalg.cholesky(gram)
    inverse = lax.linalg.triangular_solve(
        lower, jnp.eye(gram.shape[0], dtype=F32), left_side=True, lower=True
    )
    return jnp.dot(values, inverse.T, precision=lax.Precision.HIGHEST)


def sum_over(value, axis):
    n = lax.axis_size(axis)
    if n & (n - 1):
        return lax.psum(value, axis)
    bit = 1
    while bit < n:
        value = value + lax.ppermute(value, axis, [(i, i ^ bit) for i in range(n)])
        bit *= 2
    return value


def plain_way(tiles, row_index, col_index, count, sketch):
    edge = tiles.shape[1]
    width_k = sketch.shape[1]
    scale_rows = math.sqrt(RB_G * edge * lax.axis_size("row"))
    omega = sketch.reshape(CB_G, edge, width_k)
    first = tile_product(tiles, row_index, col_index, count, omega, RB_G, False)
    first = first.reshape(RB_G * edge, width_k)
    whole = sum_over(first, "col")
    gram = sum_over(gram_of(whole), "row")
    whole_float = orthonormal(whole, gram)
    share_rows = whole.shape[0] // lax.axis_size("col")
    mine = lax.dynamic_slice_in_dim(whole_float, lax.axis_index("col") * share_rows, share_rows, 0)
    ortho_one = whole_float.astype(BF16).reshape(RB_G, edge, width_k)
    cross = tile_product(tiles, col_index, row_index, count, ortho_one, CB_G, True)
    cross = cross.reshape(CB_G * edge, width_k)
    cross_full = sum_over(cross, "row").astype(BF16).reshape(CB_G, edge, width_k)
    second = tile_product(tiles, row_index, col_index, count, cross_full, RB_G, False)
    second = second.reshape(RB_G * edge, width_k)
    second = sum_over(second, "col")
    second_share = lax.dynamic_slice_in_dim(second, lax.axis_index("col") * share_rows, share_rows, 0)
    gram_two = sum_over(gram_of(second), "row")
    return mine * scale_rows, orthonormal(second_share, gram_two) * scale_rows


class Order:
    def __init__(self):
        self.token = None

    def run(self, kernel, outs, operands, specs, name, limit=12, scratch=(), aliases=None):
        n_in, n_out = len(operands), len(outs)
        tokens = () if self.token is None else (self.token,)

        def ordered(*refs):
            results = refs[n_in + len(tokens) :]
            results[n_out][...] = jnp.zeros(results[n_out].shape, F32)
            kernel(*refs[:n_in], *results[:n_out], *results[n_out + 1 :])

        *results, self.token = pl.pallas_call(
            ordered,
            out_shape=[*outs, jax.ShapeDtypeStruct((8, 128), F32)],
            in_specs=list(specs) + [ANYWHERE] * len(tokens),
            out_specs=[IN_VMEM] * (n_out + 1),
            scratch_shapes=list(scratch),
            input_output_aliases=aliases or {},
            compiler_params=pltpu.CompilerParams(vmem_limit_bytes=limit * MIB),
            cost_estimate=SMALL,
            name=name,
        )(*operands, *tokens)
        return results


def exact(a, b, ca=1, cb=0):
    return lax.dot_general(
        a, b, (((ca,), (cb,)), ((), ())), precision=lax.Precision.HIGHEST, preferred_element_type=F32
    )


def dense_first_kernel(
    core_ref, rows_ref, cols_ref, count_ref, tiles_ref, sketch_ref, *refs, chunks, pieces
):
    slabs, outs = refs[:pieces], refs[pieces : pieces + 2 * chunks]
    slab_ref, turned_ref, sem, out_sems = refs[pieces + 2 * chunks :]
    _, height, piece = slab_ref.shape
    edge = tiles_ref.shape[1]
    per = piece // edge

    def clear(i, carry):
        for p in range(pieces):
            slab_ref[p, pl.ds(pl.multiple_of(i * edge, edge), edge), :] = jnp.zeros((edge, piece), slab_ref.dtype)
        return carry

    lax.fori_loop(0, height // edge, clear, 0)
    count = count_ref[0]

    def place(t):
        r = pl.multiple_of(rows_ref[t] * edge, edge)
        c = cols_ref[t]
        at = pl.multiple_of(lax.rem(c, per) * edge, edge)
        return pltpu.make_async_copy(
            tiles_ref.at[t], slab_ref.at[lax.div(c, per), pl.ds(r, edge), pl.ds(at, edge)], sem
        )

    def start(t, carry):
        place(t).start()
        return carry

    def start_four(i, carry):
        for j in range(4):
            place(4 * i + j).start()
        return carry

    lax.fori_loop(0, lax.div(count, 4), start_four, 0)
    lax.fori_loop(4 * lax.div(count, 4), count, start, 0)
    for j in range(pieces * per):
        turned_ref[:, j * edge : (j + 1) * edge] = sketch_ref[j * edge : (j + 1) * edge, :].T
    bit = 1
    while bit <= tiles_ref.shape[0]:

        @pl.when(lax.rem(lax.div(count, bit), 2) == 1)
        def _(bit=bit):
            some = tiles_ref.at[pl.ds(0, bit)]
            pltpu.make_async_copy(some, some, sem).wait()

        bit *= 2
    writes = [
        pltpu.make_async_copy(slab_ref.at[p], slabs[p], out_sems.at[p]) for p in range(pieces)
    ]
    for write in writes:
        write.start()
    core = core_ref[0]
    pairs, k, share = outs[0].shape

    def step(j, carry):
        for side in range(2):
            i = 2 * j + (core if side == 0 else 1 - core)
            at = pl.ds(pl.multiple_of(i * share, share), share)
            value = None
            for p in range(pieces):
                block = slab_ref[p, at, :]
                term = lax.dot_general(
                    turned_ref[:, p * piece : (p + 1) * piece],
                    block,
                    (((1,), (1,)), ((), ())),
                    preferred_element_type=F32,
                )
                value = term if value is None else value + term
            for c in range(chunks):
                outs[2 * c + side][j] = value[c * k : (c + 1) * k]
        return carry

    lax.fori_loop(0, pairs, step, 0)
    for write in writes:
        write.wait()


def split_kernel(core_ref, mine_ref, other_ref, out_ref):
    pairs, k, share = mine_ref.shape
    core = core_ref[0]
    for i in range(pairs):
        for parity, ref in ((core, mine_ref), (1 - core, other_ref)):
            value = ref[i]
            high = value.astype(BF16)
            at = pl.ds(pl.multiple_of((2 * i + parity) * share, share), share)
            out_ref[:k, at] = high
            out_ref[k:, at] = (value - high.astype(F32)).astype(BF16)


def lower_blocks(rows):
    h = rows.shape[0] // 2
    left = exact(rows, rows[:h], 1, 1)
    return jnp.concatenate([left, exact(rows[h:], rows[h:], 1, 1)], axis=0)


def gram_one_kernel(*refs):
    out_ref = refs[-1]

    def of(ref, i):
        return lower_blocks(ref[i])

    out_ref[...] = jnp.zeros(out_ref.shape, F32)

    def step(i, carry):
        out_ref[...] += of(refs[0], i) + of(refs[1], i)
        return carry

    lax.fori_loop(0, refs[0].shape[0], step, 0)


def gram_kernel(blocks_ref, out_ref):
    out_ref[...] = jnp.zeros(out_ref.shape, F32)

    def step(i, carry):
        out_ref[...] += lower_blocks(blocks_ref[i])
        return carry

    lax.fori_loop(0, blocks_ref.shape[0], step, 0)


def cross_kernel(split_ref, slab_ref, out_ref):
    k, width = out_ref.shape
    step = min(512, width)

    def part(i, carry):
        at = pl.ds(pl.multiple_of(i * step, step), step)
        both = jnp.dot(split_ref[...], slab_ref[:, at], preferred_element_type=F32)
        out_ref[:, at] = both[:k] + both[k:]
        return carry

    lax.fori_loop(0, width // step, part, 0)


def pick_kernel(role_ref, *refs, n, has_received):
    received = refs[n] if has_received else None
    out_ref = refs[-1]
    for role in range(n):

        @pl.when(role_ref[0] == role)
        def _(role=role):
            value = refs[role][...]
            if has_received and role > 0:
                value = value + received[...].astype(F32)
            out_ref[...] = value.astype(out_ref.dtype)


def send_on_kernel(role_ref, *refs, n):
    for role in range(n):

        @pl.when(role_ref[0] == role)
        def _(role=role):
            refs[-1][...] = (refs[role][...] + refs[n][...].astype(F32)).astype(refs[-1].dtype)


def second_kernel(core_ref, role_ref, own_ref, slab_ref, *refs, n, has_base):
    even_refs, odd_refs = refs[:n], refs[n : 2 * n]
    bases = refs[2 * n : 2 * n + 2] if has_base else (None, None)
    at = 2 * n + 2 * has_base
    outs, total_ref = refs[at : at + 2], refs[at + 2]
    k = own_ref.shape[0]
    pairs, _, share = outs[0].shape
    core = core_ref[0]
    for role in range(n):

        @pl.when(role_ref[0] == role)
        def _(role=role):
            total = own_ref[...] + even_refs[role][...].astype(F32) + odd_refs[role][...].astype(F32)
            high = total.astype(BF16)
            total_ref[:k, :] = high
            total_ref[k:, :] = (total - high.astype(F32)).astype(BF16)

    def step(j, carry):
        for side in range(2):
            i = 2 * j + (core if side == 0 else 1 - core)
            block = slab_ref[pl.ds(pl.multiple_of(i * share, share), share), :]
            both = lax.dot_general(
                total_ref[...], block, (((1,), (1,)), ((), ())), preferred_element_type=F32
            )
            value = both[:k] + both[k:]
            outs[side][j] = bases[side][j] + value if has_base else value
        return carry

    lax.fori_loop(0, pairs, step, 0, unroll=2)


def add_kernel(*refs, n):
    for i in range(n):
        refs[2 * n + i][...] = refs[2 * i][...] + refs[2 * i + 1][...]


def encode(blocks, low_ref, high_ref):
    h = low_ref.shape[0]
    share = blocks[0].shape[1]
    most = functools.reduce(jnp.maximum, [jnp.max(jnp.abs(v), axis=1, keepdims=True) for v in blocks])
    power = jnp.ceil(jnp.log2(jnp.maximum(most, 1e-36) * (1.0 / CODE_MAX)))
    inverse = jnp.exp2(-power)
    for i, v in enumerate(blocks):
        code = jnp.round(v * inverse).astype(jnp.int32).astype(jnp.int16)
        at = slice(i * share, (i + 1) * share)
        low_ref[:, at] = code[:h]
        high_ref[:, at] = code[h:]
    tail = slice(len(blocks) * share, low_ref.shape[1])
    width = low_ref.shape[1] - len(blocks) * share
    power = jnp.broadcast_to(power, (2 * h, width)).astype(jnp.int32).astype(jnp.int16)
    low_ref[:, tail] = power[:h]
    high_ref[:, tail] = power[h:]


def decode(ref, pairs, share):
    power = ref[:, pairs * share : pairs * share + 128].astype(jnp.int32).astype(F32)
    factor = jnp.exp2(jnp.max(power, axis=1, keepdims=True))
    return [
        ref[:, i * share : (i + 1) * share].astype(jnp.int32).astype(F32) * factor for i in range(pairs)
    ]


def code_first_kernel(a_ref, b_ref, low_ref, high_ref):
    encode([a_ref[i] + b_ref[i] for i in range(a_ref.shape[0])], low_ref, high_ref)


def decoded_sums(refs, pairs, share):
    low, low_more, high, high_more = [decode(ref, pairs, share) for ref in refs]
    return [
        jnp.concatenate([low[i] + low_more[i], high[i] + high_more[i]], axis=0) for i in range(pairs)
    ]


def code_next_kernel(*refs, pairs, share):
    encode(decoded_sums(refs[:4], pairs, share), refs[4], refs[5])


def code_last_kernel(*refs):
    out_ref = refs[4]
    for i, v in enumerate(decoded_sums(refs[:4], out_ref.shape[0], out_ref.shape[2])):
        out_ref[i] = v


def keep_give_kernel(core_ref, value_ref, keep_ref, give_ref):
    h = keep_ref.shape[0]
    core = core_ref[0]
    keep_ref[...] = value_ref[pl.ds(pl.multiple_of(core * h, h), h), :]
    give_ref[...] = value_ref[pl.ds(pl.multiple_of((1 - core) * h, h), h), :]


def whole_of(core_ref, mine, other):
    core = core_ref[0] == 0
    return jnp.concatenate([jnp.where(core, mine, other), jnp.where(core, other, mine)], axis=0)


def chol_inverse(a, step):
    n = a.shape[0]
    rows = lax.broadcasted_iota(jnp.int32, (n, n), 0)
    lanes = lax.broadcasted_iota(jnp.int32, (n, n), 1)
    lane = lax.broadcasted_iota(jnp.int32, (1, n), 1)
    pivots = jnp.ones((1, n), F32)
    done = []
    for k in range(0, n, step):
        m = a.shape[0]
        cols = [jnp.broadcast_to(a[:, k + j : k + j + 1], (m, n)) for j in range(step)]
        s = [[cols[q][j : j + 1, :] for q in range(step)] for j in range(step)]
        r = [a[j : j + 1, :] for j in range(step)]
        update = None
        for j in range(step):
            inverse = 1.0 / s[j][j]
            pivots = jnp.where(lane == k + j, s[j][j], pivots)
            row = r[j] + jnp.where(lane == k + j, s[j][j], 0.0)
            for q in range(j + 1, step):
                factor = s[q][j] * inverse
                r[q] = r[q] - factor * row
                for p in range(j + 1, step):
                    s[q][p] = s[q][p] - factor * s[j][p]
            column = cols[j] * inverse
            for q in range(j + 1, step):
                cols[q] = cols[q] - column * s[j][q]
            update = column * row if update is None else update + column * row
        done.extend(r)
        if m > step:
            a = a[step:] - update[step:]
    full = jnp.concatenate(done, 0)
    root = jnp.broadcast_to(lax.rsqrt(pivots), (n, n))
    by_row = jnp.sum(jnp.where(rows == lanes, root, 0.0), axis=1, keepdims=True)
    return jnp.where(lanes <= rows, full * (1.0 / pivots) * by_row, 0.0)


def check_of(squares, diagonals):
    k = sum(d.shape[1] for d in diagonals)
    gain = jnp.sum(jnp.sum(squares, axis=1, keepdims=True), axis=0, keepdims=True) / k
    good = gain < GAIN_MAX
    for diagonal in diagonals:
        good &= (jnp.min(diagonal, axis=1, keepdims=True) > DIAG_MIN) & (
            jnp.max(diagonal, axis=1, keepdims=True) < DIAG_MAX
        )
    return jnp.broadcast_to(jnp.where(good, 1.0, 0.0), (8, 128))


def diagonal_of(gram):
    k = gram.shape[0]
    rows = lax.broadcasted_iota(jnp.int32, (k, k), 0)
    lanes = lax.broadcasted_iota(jnp.int32, (k, k), 1)
    return jnp.sum(jnp.where(rows == lanes, gram, 0.0), axis=0, keepdims=True)


def range_top_kernel(core_ref, mine_ref, other_ref, share_ref, gram_ref, top_ref, rows_ref):
    gram = whole_of(core_ref, mine_ref[...], other_ref[...])
    gram_ref[...] = gram
    h = top_ref.shape[0]
    top = chol_inverse(gram[:h], 8)
    top_ref[...] = top
    rows_ref[...] = exact(top, share_ref[:h, :])


def rest_of_basis(gram, top, top_rows, share, out_ref, scale):
    h = top.shape[0]
    side = exact(gram[h : 2 * h], top, 1, 1)
    rest = gram[2 * h :] - exact(side, side, 1, 1)
    left = share - exact(side, top_rows)
    out_ref[:, :h] = top_rows.T * scale
    low = chol_inverse(rest, 8)
    out_ref[:, h:] = exact(left, low, 0, 1) * scale
    corner = exact(exact(low, side), top)
    first, second = diagonal_of(gram[:h]), diagonal_of(gram[2 * h :])
    squares = (top * top + corner * corner) * first + low * low * second
    return check_of(squares, (first, second))


def range_rest_kernel(gram_ref, top_ref, rows_ref, share_ref, out_ref, check_ref, *, scale):
    h = top_ref.shape[0]
    check_ref[...] = rest_of_basis(
        gram_ref[...], top_ref[...], rows_ref[...], share_ref[h:, :], out_ref, scale
    )


def basis_kernel(core_ref, mine_ref, other_ref, share_ref, before_ref, out_ref, check_ref, *, scale):
    gram = whole_of(core_ref, mine_ref[...], other_ref[...])
    h = gram.shape[1]
    top = chol_inverse(gram[:h], 8)
    rows = exact(top, share_ref[:h, :])
    check = rest_of_basis(gram, top, rows, share_ref[h:, :], out_ref, scale)
    check_ref[...] = check * before_ref[...]


def tie(value, tokens):
    return lax.optimization_barrier((value, *tokens))[0] if tokens else value


def swap(value, axis, bit):
    n = lax.axis_size(axis)
    return lax.ppermute(value, axis, [(i, i ^ bit) for i in range(n)])


def bits_of(n, first):
    bits = []
    bit = first
    while bit < n:
        bits.append(bit)
        bit *= 2
    return bits


def sum_over_chips(order, keep, give):
    pairs, k, share = keep.shape
    bits = bits_of(lax.axis_size("col"), 2)
    message = jax.ShapeDtypeStruct((k // 2, pairs * share + 128), jnp.int16)
    received = swap(give, "col", 1)
    yield
    halves = order.run(code_first_kernel, [message, message], (keep, received), (IN_VMEM,) * 2, "code_cores")
    for level in range(len(bits)):
        moved = [swap(v, "col", bits[(level + t) % len(bits)]) for t, v in enumerate(halves)]
        yield
        operands = (halves[0], moved[0], halves[1], moved[1])
        if level < len(bits) - 1:
            halves = order.run(
                functools.partial(code_next_kernel, pairs=pairs, share=share),
                [message, message],
                operands,
                (IN_VMEM,) * 4,
                "code_chips",
            )
        else:
            (total,) = order.run(
                code_last_kernel, [jax.ShapeDtypeStruct(keep.shape, F32)], operands, (IN_VMEM,) * 4, "sum_chips"
            )
    return total


def sum_over_rows(order, half):
    for bit in bits_of(lax.axis_size("row"), 1):
        other = swap(half, "row", bit)
        yield
        (half,) = order.run(
            functools.partial(add_kernel, n=1),
            [jax.ShapeDtypeStruct(half.shape, F32)],
            (half, other),
            (IN_VMEM,) * 2,
            "sum_rows",
        )
    return half, swap(half, "col", 1)


def keep_and_give(order, core, gram):
    half = jax.ShapeDtypeStruct((gram.shape[0] // 2, gram.shape[1]), F32)
    return order.run(keep_give_kernel, [half, half], (core, gram), (IN_SMEM, IN_VMEM), "gram_halves")


def sum_over_all(order, core, gram):
    keep, give = keep_and_give(order, core, gram)
    received = swap(give, "col", 1)
    yield
    (half,) = order.run(
        functools.partial(add_kernel, n=1),
        [jax.ShapeDtypeStruct(keep.shape, F32)],
        (keep, received),
        (IN_VMEM,) * 2,
        "sum_gram_cores",
    )
    half, other = yield from sum_over_rows(order, half)
    yield
    return half, other


class Jobs:
    def __init__(self):
        self.active = []

    def add(self, steps):
        self.active.append(steps)
        return self.advance(steps)

    def advance(self, steps):
        try:
            next(steps)
        except StopIteration:
            self.active.remove(steps)

    def step(self):
        for steps in list(self.active):
            self.advance(steps)

    def finish(self):
        while self.active:
            self.step()


def scan_rows(order, jobs, splits, done, last, slab, core, k, pairs, share):
    n = lax.axis_size("row")
    roles = n // 2
    i = lax.axis_index("row")
    even = (i % 2) == 0
    hop_even = jnp.where(even, i, n - 1 - i)
    hop_odd = jnp.where(even, n - 1 - i, i)
    role_even = (hop_even // 2).astype(jnp.int32)[None]
    role_odd = jnp.minimum((hop_odd - 1) // 2, max(roles - 2, 0)).astype(jnp.int32)[None]
    role_sum = (jnp.where(even, n - 2 - i, i - 1) // 2).astype(jnp.int32)[None]
    pairs_even = [(j, j ^ 1) for j in range(n)]
    pairs_odd = [(j, j + 1) for j in range(1, n - 1, 2)] + [(j + 1, j) for j in range(1, n - 1, 2)]
    chunks = len(done)
    per = len(slab)
    height, piece = slab[0].shape
    m = chunks * per
    own = {}

    def own_of(q):
        q = min(max(q, 0), m - 1)
        if q not in own:
            while q // per not in splits:
                jobs.step()
            (own[q],) = order.run(
                cross_kernel,
                [jax.ShapeDtypeStruct((k, piece), F32)],
                (splits[q // per], slab[q % per]),
                (IN_VMEM, IN_VMEM),
                "cross_piece",
            )
        return own[q]

    sent_even, sent_odd = {}, {}
    n_even = m + (roles - 1) * LAG
    n_odd = m + (roles - 2) * LAG if roles > 1 else 0
    message = [jax.ShapeDtypeStruct((k, piece), BF16)]

    def send_even(s):
        if s >= n_even or s in sent_even:
            return
        owns = [own_of(s - role * LAG) for role in range(roles)]
        received = sent_odd.get(s - LAG)
        operands = (role_even, *owns) + ((received,) if received is not None else ())
        (value,) = order.run(
            functools.partial(pick_kernel, n=roles, has_received=received is not None),
            message,
            operands,
            (IN_SMEM,) + (IN_VMEM,) * (len(operands) - 1),
            "send_even",
        )
        sent_even[s] = lax.ppermute(value, "row", pairs_even)

    def send_odd(s):
        if not 0 <= s < n_odd:
            return
        owns = [own_of(s - role * LAG) for role in range(roles - 1)]
        (value,) = order.run(
            functools.partial(send_on_kernel, n=roles - 1),
            message,
            (role_odd, *owns, sent_even[s]),
            (IN_SMEM,) + (IN_VMEM,) * roles,
            "send_odd",
        )
        sent_odd[s] = lax.ppermute(value, "row", pairs_odd)

    seconds = [None] * chunks
    nothing = jnp.zeros((k, piece), BF16)

    def odd_for(q, role):
        hop = n - 3 - 2 * role
        return nothing if hop < 0 else sent_odd[q + ((hop - 1) // 2) * LAG]

    def product(q):
        if not 0 <= q < m:
            return
        evens = [sent_even[q + role * LAG] for role in range(roles)]
        odds = [odd_for(q, role) for role in range(roles)]
        base = seconds[q // per]
        has_base = base is not None
        operands = (core, role_sum, own_of(q), slab[q % per], *evens, *odds, *(base or ()))
        seconds[q // per] = order.run(
            functools.partial(second_kernel, n=roles, has_base=has_base),
            [jax.ShapeDtypeStruct((pairs, k, share), F32)] * 2,
            operands,
            (IN_SMEM, IN_SMEM) + (IN_VMEM,) * (len(operands) - 2),
            "second_piece",
            scratch=(pltpu.VMEM((2 * k, piece), BF16),),
            aliases={len(operands) - 2: 0, len(operands) - 1: 1} if has_base else None,
        )
        if q % per == per - 1:
            done[q // per](*seconds[q // per])

    send_even(0)
    for s in range(n_even):
        need = s + 1 - LAG
        if need < 0 or need in sent_odd or need >= n_odd:
            send_even(s + 1)
        send_odd(s)
        send_even(s + 1)
        if s == max(n_even - 3, 0):
            last()
        jobs.step()
        product(s - (roles - 1) * LAG)


def body(tile_data, tile_rows, tile_cols, tile_count, sketch):
    tiles = tile_data[0, 0]
    row_index = tile_rows[0, 0]
    col_index = tile_cols[0, 0]
    count = tile_count[0]
    edge = tiles.shape[1]
    k = sketch.shape[1]
    height, width = RB_G * edge, CB_G * edge
    shares = lax.axis_size("col")
    pairs = shares // 2
    share = height // shares
    scale = math.sqrt(height * lax.axis_size("row"))
    me = lax.axis_index("col")
    core = (me % 2).astype(jnp.int32)[None]
    order, jobs = Order(), Jobs()

    part = jax.ShapeDtypeStruct((pairs, k, share), F32)
    piece = width // PIECES
    slab_and_parts = pl.pallas_call(
        functools.partial(dense_first_kernel, chunks=CHUNKS, pieces=PIECES),
        out_shape=[pltpu.HBM((height, piece), BF16)] * PIECES + [part] * (2 * CHUNKS),
        in_specs=[IN_SMEM] * 4 + [ANYWHERE, IN_VMEM],
        out_specs=[IN_HBM] * PIECES + [IN_VMEM] * (2 * CHUNKS),
        scratch_shapes=[
            pltpu.VMEM((PIECES, height, piece), BF16),
            pltpu.VMEM((k, width), BF16),
            pltpu.SemaphoreType.DMA,
            pltpu.SemaphoreType.DMA((PIECES,)),
        ],
        compiler_params=pltpu.CompilerParams(vmem_limit_bytes=24 * MIB),
        cost_estimate=SMALL,
        name="dense_first",
    )(core, row_index, col_index, count, tiles, sketch)
    slab, parts = slab_and_parts[:PIECES], slab_and_parts[PIECES:]

    def own_rows(blocks):
        return lax.dynamic_index_in_dim(blocks, me // 2, 0, keepdims=False)

    ready = jax.ShapeDtypeStruct((8, 128), F32)
    out = jax.ShapeDtypeStruct((share, k), F32)
    h = k // 2
    packed = jax.ShapeDtypeStruct((3 * h, h), F32)
    first, splits, result = [], {}, {}

    def first_sum():
        total = yield from sum_over_chips(order, *parts)
        other = swap(total, "col", 1)
        yield
        first.extend((total, other))
        (splits[0],) = order.run(
            split_kernel,
            [jax.ShapeDtypeStruct((2 * k, height), BF16)],
            (core, total, other),
            (IN_SMEM, IN_VMEM, IN_VMEM),
            "split",
        )

    def range_one():
        yield
        yield
        yield
        (gram,) = order.run(
            gram_one_kernel, [packed], first, (IN_VMEM,) * 2, "gram_one"
        )
        keep, _ = keep_and_give(order, core, gram)
        while "last" not in result:
            yield
        half, other = yield from sum_over_rows(order, keep)
        rows = own_rows(first[0])
        yield
        gram, top, top_rows = order.run(
            range_top_kernel,
            [packed, jax.ShapeDtypeStruct((h, h), F32), jax.ShapeDtypeStruct((h, share), F32)],
            (core, half, other, rows),
            (IN_SMEM,) + (IN_VMEM,) * 3,
            "range_top",
        )
        yield
        result["range"] = order.run(
            functools.partial(range_rest_kernel, scale=scale),
            [out, ready],
            (gram, top, top_rows, rows),
            (IN_VMEM,) * 4,
            "range_rest",
        )

    def basis_of(keep, give):
        total = yield from sum_over_chips(order, keep, give)
        (gram,) = order.run(gram_kernel, [packed], (total,), (IN_VMEM,), "gram_two")
        half, other = yield from sum_over_all(order, core, gram)
        while "range" not in result:
            yield
        result["basis"] = order.run(
            functools.partial(basis_kernel, scale=scale),
            [out, ready],
            (core, half, other, own_rows(total), result["range"][1]),
            (IN_SMEM,) + (IN_VMEM,) * 4,
            "basis",
        )

    def finished(keep, give):
        steps = basis_of(keep, give)
        jobs.active.insert(0, steps)
        jobs.advance(steps)

    jobs.add(first_sum())
    jobs.finish()
    jobs.add(range_one())
    scan_rows(order, jobs, splits, [finished], lambda: result.update(last=True), slab, core, k, pairs, share)
    jobs.finish()
    range_out = result["range"][0]
    basis, check = result["basis"]
    return lax.cond(
        check[0, 0] > 0.5,
        lambda: (range_out, basis),
        lambda: plain_way(tiles, row_index, col_index, tile_count[0, 0], sketch),
    )


def solution(mesh):
    placed = (
        P("row", "col", None, None, None),
        P("row", "col", None),
        P("row", "col", None),
        P("row", "col"),
        P("col", None),
    )
    return jax.shard_map(
        body,
        mesh=mesh,
        in_specs=placed,
        out_specs=(P(("row", "col"), None), P(("row", "col"), None)),
        check_vma=False,
    )
```
